32 devices in a mesh: replica: 2 (over y), row: 4 (over x, core), col: 4 (over z).
Axes of the slice: x: 2, y: 2, z: 4, core: 2. Of those that a mesh axis runs over, the one named last changes fastest.
Arguments:
- pair: bfloat16 [256, 128, 128], P(('replica', 'row'), 'col'), parts along dimension 0, may hold values from -6 to 6
- cotangent: bfloat16 [256, 128, 128], P(('replica', 'row'), 'col'), parts along dimension 0, may hold values from -6 to 6
- valid: int32 [256], P('replica'), parts along dimension 0, may hold values from 0 to 1, as said below
- in_gain: float32 [128], replicated, may hold values from 0.1 to 1.9
- proj_weight: bfloat16 [128, 512], replicated, may hold values from -0.5 to 0.5
- gate_weight: bfloat16 [128, 128], replicated, may hold values from -0.5 to 0.5
- out_gain: float32 [128], replicated, may hold values from 0.1 to 1.9
- out_weight: bfloat16 [128, 128], replicated, may hold values from -0.5 to 0.5
Outputs:
- update: bfloat16 [256, 128, 128], P(('replica', 'row'), 'col'), parts along dimension 0
- pair_grad: float32 [256, 128, 128], P(('replica', 'row'), 'col'), parts along dimension 0
The draws below stay inside these ranges and needn't reach their ends.
There are 2 independent parts, one for each index of `replica`. The reference program is written for one: setup_inputs(seed, part) draws one part's arguments, and reference() takes and returns one part's arrays. A program takes and returns all parts, laid end to end along the dimension named above; an argument that names none is the same for every part. Nothing has to cross between parts.
Inputs may be any that keep to these rules, and one draw needn't show every extreme that they name: valid is 0 on a trailing run of padding that ends at the last token, and 1 on the first token; some tokens before the padding are masked too.
All inputs are finite; a program needn't handle non-finite values.
Results may differ from the reference program's by a relative error of at most 0.0079.
Values may be sent and summed in bfloat16 or wider, within the bound.
No kernel may reach another device: no remote copies, remote signals or barrier semaphores. Data moves between devices by JAX's collectives and lax.ppermute only.
A program may use at most 128 MiB of HBM per device.

```python
import jax
import jax.numpy as jnp
from jax import lax

C = 128
H = 128
N = 128


def draw_valid(key, part):
    key = jax.random.fold_in(key, 7)
    length_key = jax.random.fold_in(key, 11)
    token_key = jax.random.fold_in(key, 13)
    limit = jax.random.randint(length_key, (), 3 * N // 4, N)
    places = jnp.arange(N)
    present = jax.random.randint(token_key, (N,), 0, 4)
    inside = (places < limit).astype(jnp.int32)
    resolved = jnp.where(present > 0, 1, 0).astype(jnp.int32)
    resolved = jnp.where(places == 0, 1, resolved).astype(jnp.int32)
    return (inside * resolved).astype(jnp.int32)


def level_of(key, dims, pieces, low, top_value):
    def one(axis_at, shards_of):
        heights = jax.random.uniform(jax.random.fold_in(jax.random.fold_in(key, 6), axis_at), (shards_of,), jnp.float32, low / len(pieces), top_value / len(pieces))
        return jnp.repeat(jnp.exp(heights), dims[axis_at] // shards_of).reshape((-1,) + (1,) * (len(dims) - axis_at - 1))

    loudness = one(*pieces[0])
    for cut in pieces[1:]:
        loudness = loudness * one(*cut)
    return loudness


def gaussian(stream_key, shape, deviation, bound, split=(), held_as=jnp.bfloat16):
    values = deviation * jax.random.normal(stream_key, shape, jnp.float32)
    if split:
        values = values * level_of(stream_key, shape, split, -0.22, 0.18)
    return jnp.clip(values, -bound, bound).astype(held_as)


def setup_inputs(seed: int = 0, part: int = 0) -> dict:
    keys = jax.random.split(jax.random.key(seed), 9)
    own_keys = jax.random.split(jax.random.fold_in(keys[8], part), 9)
    pair = gaussian(own_keys[0], (N, N, C), 1.0, 6.0, ((0, 4), (1, 4)))
    cotangent = gaussian(own_keys[1], (N, N, C), 1.0, 6.0, ((0, 4), (1, 4)))
    valid = draw_valid(jax.random.fold_in(jax.random.fold_in(keys[8], part), 71), part)
    in_gain = jnp.clip(1.0 + 0.18 * jax.random.normal(keys[3], (C,), jnp.float32), 0.1, 1.9)
    proj_weight = gaussian(keys[4], (C, 4 * H), C ** -0.5, 0.5)
    gate_weight = gaussian(keys[5], (C, C), C ** -0.5, 0.5)
    out_gain = jnp.clip(1.0 + 0.18 * jax.random.normal(keys[6], (H,), jnp.float32), 0.1, 1.9)
    out_weight = gaussian(keys[7], (H, C), H ** -0.5, 0.5)
    return dict(pair=pair, cotangent=cotangent, valid=valid, in_gain=in_gain, proj_weight=proj_weight, gate_weight=gate_weight, out_gain=out_gain, out_weight=out_weight)


eps_norm = 1e-05

def layer_norm(values, gain):
    mean_val = lax.optimization_barrier(jnp.mean(values, axis=-1, keepdims=True))
    centred = values - mean_val
    inv_std = lax.rsqrt(lax.optimization_barrier(jnp.mean(centred * centred, axis=-1, keepdims=True)) + eps_norm)
    unit = centred * inv_std
    return (unit * gain, unit, inv_std)

def norm_back(grad_unit, unit, inv_std):
    first = lax.optimization_barrier(jnp.mean(grad_unit, axis=-1, keepdims=True))
    second = lax.optimization_barrier(jnp.mean(grad_unit * unit, axis=-1, keepdims=True))
    return inv_std * (grad_unit - first - unit * second)

def reference(pair, cotangent, valid, in_gain, proj_weight, gate_weight, out_gain, out_weight):
    normed_f, unit_in, inv_in = layer_norm(pair.astype(jnp.float32), in_gain)
    normed = normed_f.astype(jnp.bfloat16)
    flat = normed.reshape(N * N, C)
    proj = jnp.dot(flat, proj_weight, preferred_element_type=jnp.float32).reshape(N, N, 4 * H)
    keeper = valid.astype(jnp.float32)
    pair_keep = (keeper[:, None] * keeper[None, :])[:, :, None]
    left_sig = jax.nn.sigmoid(proj[..., :H])
    left_val = proj[..., H:2 * H]
    right_sig = jax.nn.sigmoid(proj[..., 2 * H:3 * H])
    right_val = proj[..., 3 * H:]
    left = (left_sig * left_val * pair_keep).astype(jnp.bfloat16)
    right = (right_sig * right_val * pair_keep).astype(jnp.bfloat16)
    tri = jnp.einsum('ikh,jkh->ijh', left.astype(jnp.float32), right.astype(jnp.float32), precision=lax.Precision.HIGHEST)
    tnorm_f, unit_tri, inv_tri = layer_norm(tri, out_gain)
    tnorm = tnorm_f.astype(jnp.bfloat16)
    gate = jax.nn.sigmoid(jnp.dot(flat, gate_weight, preferred_element_type=jnp.float32)).reshape(N, N, C)
    lin = jnp.dot(tnorm.reshape(N * N, H), out_weight, preferred_element_type=jnp.float32).reshape(N, N, C)
    update = (gate * lin).astype(jnp.bfloat16)
    cot = cotangent.astype(jnp.float32)
    d_lin = (cot * gate).astype(jnp.bfloat16)
    d_gpre = (cot * lin * gate * (1.0 - gate)).astype(jnp.bfloat16)
    d_tnorm = jnp.dot(d_lin.reshape(N * N, C), out_weight.T, preferred_element_type=jnp.float32).reshape(N, N, H)
    d_tri = norm_back(d_tnorm * out_gain, unit_tri, inv_tri).astype(jnp.bfloat16)
    d_left = jnp.einsum('ijh,jkh->ikh', d_tri.astype(jnp.float32), right.astype(jnp.float32), precision=lax.Precision.HIGHEST)
    d_right = jnp.einsum('ijh,ikh->jkh', d_tri.astype(jnp.float32), left.astype(jnp.float32), precision=lax.Precision.HIGHEST)
    d_proj = jnp.concatenate([d_left * pair_keep * left_val * left_sig * (1.0 - left_sig), d_left * pair_keep * left_sig, d_right * pair_keep * right_val * right_sig * (1.0 - right_sig), d_right * pair_keep * right_sig], axis=-1).astype(jnp.bfloat16)
    d_normed = jnp.dot(d_proj.reshape(N * N, 4 * H), proj_weight.T, preferred_element_type=jnp.float32)
    d_normed = d_normed + jnp.dot(d_gpre.reshape(N * N, C), gate_weight.T, preferred_element_type=jnp.float32)
    pair_grad = norm_back(d_normed.reshape(N, N, C) * in_gain, unit_in, inv_in)
    return (update, pair_grad)
```

```python
import functools

import jax
import jax.numpy as jnp
from jax import lax
from jax.experimental import pallas as pl
from jax.experimental.pallas import tpu as pltpu
from jax.sharding import PartitionSpec as P

eps_norm = 1e-05


def layer_norm(values, gain):
    mean_val = jnp.mean(values, axis=-1, keepdims=True)
    centred = values - mean_val
    inv_std = lax.rsqrt(jnp.mean(centred * centred, axis=-1, keepdims=True) + eps_norm)
    unit = centred * inv_std
    return (unit * gain, unit, inv_std)


def norm_back(grad_unit, unit, inv_std):
    first = jnp.mean(grad_unit, axis=-1, keepdims=True)
    second = jnp.mean(grad_unit * unit, axis=-1, keepdims=True)
    return inv_std * (grad_unit - first - unit * second)


def on_device(pair, cotangent, valid, in_gain, proj_weight, gate_weight, out_gain, out_weight):
    tile_rows = pair.shape[0]
    channels = pair.shape[2]
    hidden = out_weight.shape[0]
    cells = tile_rows * tile_rows
    keeper = valid.astype(jnp.float32)
    row_keep = lax.dynamic_slice_in_dim(keeper, lax.axis_index("row") * tile_rows, tile_rows)
    col_keep = lax.dynamic_slice_in_dim(keeper, lax.axis_index("col") * tile_rows, tile_rows)
    pair_keep = (row_keep[:, None] * col_keep[None, :])[:, :, None]
    normed_f, unit_in, inv_in = layer_norm(pair.astype(jnp.float32), in_gain)
    normed = normed_f.astype(jnp.bfloat16)
    flat = normed.reshape(cells, channels)
    proj = jnp.dot(flat, proj_weight, preferred_element_type=jnp.float32).reshape(
        tile_rows, tile_rows, 4 * hidden
    )
    left_sig = jax.nn.sigmoid(proj[..., :hidden])
    left_val = proj[..., hidden : 2 * hidden]
    right_sig = jax.nn.sigmoid(proj[..., 2 * hidden : 3 * hidden])
    right_val = proj[..., 3 * hidden :]
    left = (left_sig * left_val * pair_keep).astype(jnp.bfloat16)
    right = (right_sig * right_val * pair_keep).astype(jnp.bfloat16)
    panel = lax.all_gather(right, "row", axis=0, tiled=True)
    piece = panel
    tri = jnp.swapaxes(
        lax.psum_scatter(
            jnp.einsum("ikh,jkh->jih", left, piece, preferred_element_type=jnp.float32),
            "col",
            scatter_dimension=0,
            tiled=True,
        ),
        0,
        1,
    )
    tnorm_f, unit_tri, inv_tri = layer_norm(tri, out_gain)
    tnorm = tnorm_f.astype(jnp.bfloat16)
    gate = jax.nn.sigmoid(jnp.dot(flat, gate_weight, preferred_element_type=jnp.float32)).reshape(
        tile_rows, tile_rows, channels
    )
    lin = jnp.dot(
        tnorm.reshape(cells, hidden), out_weight, preferred_element_type=jnp.float32
    ).reshape(tile_rows, tile_rows, channels)
    update = (gate * lin).astype(jnp.bfloat16)
    cot = cotangent.astype(jnp.float32)
    d_lin = (cot * gate).astype(jnp.bfloat16)
    d_gpre = (cot * lin * gate * (1.0 - gate)).astype(jnp.bfloat16)
    d_tnorm = jnp.dot(
        d_lin.reshape(cells, channels), out_weight.T, preferred_element_type=jnp.float32
    ).reshape(tile_rows, tile_rows, hidden)
    d_tri = norm_back(d_tnorm * out_gain, unit_tri, inv_tri).astype(jnp.bfloat16)
    grad_rows = lax.all_gather(d_tri, "col", axis=1, tiled=True)
    back_panel = lax.all_gather(right, "row", axis=0, tiled=True)
    piece = grad_rows
    d_right = lax.psum_scatter(
        jnp.einsum("ijh,ikh->jkh", piece, left, preferred_element_type=jnp.float32),
        "row",
        scatter_dimension=0,
        tiled=True,
    )
    d_left = jnp.einsum("ijh,jkh->ikh", grad_rows, back_panel, preferred_element_type=jnp.float32)
    d_proj = jnp.concatenate(
        [
            d_left * pair_keep * left_val * left_sig * (1.0 - left_sig),
            d_left * pair_keep * left_sig,
            d_right * pair_keep * right_val * right_sig * (1.0 - right_sig),
            d_right * pair_keep * right_sig,
        ],
        axis=-1,
    ).astype(jnp.bfloat16)
    d_normed = jnp.dot(
        d_proj.reshape(cells, 4 * hidden), proj_weight.T, preferred_element_type=jnp.float32
    )
    d_normed = d_normed + jnp.dot(
        d_gpre.reshape(cells, channels), gate_weight.T, preferred_element_type=jnp.float32
    )
    pair_grad = norm_back(
        d_normed.reshape(tile_rows, tile_rows, channels) * in_gain, unit_in, inv_in
    )
    return (update, pair_grad)


F32 = jnp.float32
BF16 = jnp.bfloat16
LANES = 128


def dot(a, b, dims):
    return lax.dot_general(a, b, ((dims[:1], dims[1:]), ((), ())), preferred_element_type=F32)


def column(gain):
    n = gain.shape[1]
    return jnp.broadcast_to(gain, (n, n)).T


def spread(col, width):
    return jnp.concatenate([col] * (width // col.shape[1]), axis=1)


def unit_rows(values):
    n = values.shape[0]
    centred = values - jnp.sum(values, axis=0, keepdims=True) * (1.0 / n)
    inv = lax.rsqrt(jnp.sum(centred * centred, axis=0, keepdims=True) * (1.0 / n) + eps_norm)
    return centred * inv, inv


def unit_back(q, unit, inv):
    n = q.shape[0]
    first = jnp.sum(q, axis=0, keepdims=True) * (1.0 / n)
    second = jnp.sum(q * unit, axis=0, keepdims=True) * (1.0 / n)
    return inv * (q - first - unit * second)


def swap_blocks(a):
    width = a[0].shape[1] // 4
    lane = lax.broadcasted_iota(jnp.int32, a[0].shape, 1)
    low = lane < 2 * width
    even = (lane // width) % 2 == 0
    half = lambda x: pltpu.roll(x, 2 * width, 1)
    t0 = jnp.where(low, a[0], half(a[2]))
    t2 = jnp.where(low, half(a[0]), a[2])
    t1 = jnp.where(low, a[1], half(a[3]))
    t3 = jnp.where(low, half(a[1]), a[3])
    up = lambda x: pltpu.roll(x, width, 1)
    down = lambda x: pltpu.roll(x, 3 * width, 1)
    return (
        jnp.where(even, t0, up(t1)),
        jnp.where(even, down(t0), t1),
        jnp.where(even, t2, up(t3)),
        jnp.where(even, down(t2), t3),
    )


def keep_row(valid_ref, tile, cells):
    n = valid_ref.shape[1]
    v = jnp.broadcast_to(valid_ref[...].astype(F32), (8, n))
    token = lax.broadcasted_iota(jnp.int32, (n, cells), 0)
    cell = lax.broadcasted_iota(jnp.int32, (n, cells), 1)
    first = (token == lax.axis_index("row") * tile + cell // tile).astype(F32)
    second = (token == lax.axis_index("col") * tile + cell % tile).astype(F32)
    return (dot(v, first, (1, 0)) * dot(v, second, (1, 0)))[:1]


def normed_of(pair_ref, in_gain_ref):
    unit, inv = unit_rows(pair_ref[...].astype(F32).T)
    normed = (unit * spread(column(in_gain_ref[...]), unit.shape[1])).astype(BF16)
    return normed, unit, inv


def project_kernel(tile, pair_ref, valid_ref, in_gain_ref, proj_ref, out_ref):
    cells, channels = pair_ref.shape
    hidden = proj_ref.shape[1] // 4
    shards, both, _ = out_ref.shape
    normed, _, _ = normed_of(pair_ref, in_gain_ref)
    keep = keep_row(valid_ref, tile, cells)
    sides = []
    for side in range(2):
        weight = proj_ref[:, 2 * hidden * side : 2 * hidden * (side + 1)].T
        proj = dot(weight, normed, (1, 0))
        sides.append(jax.nn.sigmoid(proj[:hidden]) * proj[hidden:] * keep)
    for s in range(shards):
        rows = slice(s * both // 2, (s + 1) * both // 2)
        out_ref[s] = jnp.concatenate([sides[0][rows], sides[1][rows]], axis=0).astype(BF16)


def local_kernel(
    tile, pair_ref, cot_ref, valid_ref, in_gain_ref, proj_ref, gate_w_ref, out_gain_ref, out_w_ref,
    unit_ref, inv_ref, factor_ref, gate_ref, back_ref, q_ref,
):
    cells, channels = pair_ref.shape
    hidden = proj_ref.shape[1] // 4
    normed, unit, inv = normed_of(pair_ref, in_gain_ref)
    unit_ref[...] = unit
    inv_ref[...] = inv
    keep = keep_row(valid_ref, tile, cells)
    for side in range(2):
        weight = proj_ref[:, 2 * hidden * side : 2 * hidden * (side + 1)].T
        proj = dot(weight, normed, (1, 0))
        sig = jax.nn.sigmoid(proj[:hidden])
        factor_ref[2 * side] = keep * proj[hidden:] * sig * (1.0 - sig)
        factor_ref[2 * side + 1] = keep * sig
    gate = jax.nn.sigmoid(dot(gate_w_ref[...].T, normed, (1, 0)))
    cot = cot_ref[...].astype(F32).T
    gate_ref[...] = gate
    back_ref[...] = cot * gate * (1.0 - gate)
    d_lin = (cot * gate).astype(BF16)
    q_ref[...] = dot(out_w_ref[...], d_lin, (1, 0)) * spread(column(out_gain_ref[...]), cells)


def tri_kernel(grid_rows, recv_ref, left_ref, right_ref, out_ref, rows, tri):
    devices, both, cells = recv_ref.shape
    per = both // 2
    n = left_ref.shape[1]
    tile = n // grid_rows
    groups = cells // LANES
    for r in range(grid_rows):
        blocks = [recv_ref[grid_rows * r + c].astype(F32) for c in range(grid_rows)]
        for g in range(groups):
            lanes = slice(g * LANES, (g + 1) * LANES)
            for p, rows_p in enumerate(swap_blocks([b[:, lanes] for b in blocks])):
                at = (r * tile + g * grid_rows + p) * both
                rows[at : at + both, :] = rows_p
    for h in range(per):
        left = rows[pl.ds(h, n, stride=both), :].astype(BF16)
        right = rows[pl.ds(per + h, n, stride=both), :].astype(BF16)
        left_ref[h] = left
        right_ref[h] = right
        tri[pl.ds(h, n, stride=per), :] = dot(left, right, (1, 1))
    half = groups // 2
    for r in range(grid_rows):
        for g in range(half):
            parts = []
            for k in range(2):
                at = (r * tile + (g + k * half) * grid_rows) * per
                parts.append(swap_blocks([tri[at + p * per : at + (p + 1) * per, :] for p in range(grid_rows)]))
            for c in range(grid_rows):
                out_ref[grid_rows * r + c, :, g * LANES : (g + 1) * LANES] = jnp.concatenate(
                    [parts[0][c], parts[1][c]], axis=0
                ).astype(BF16)


def halves_of(recv_ref):
    shards, both, width = recv_ref.shape
    x = recv_ref[...].astype(F32)
    rows = shards * both // 2
    return jnp.concatenate(
        [x[:, : both // 2].reshape(rows, width), x[:, both // 2 :].reshape(rows, width)], axis=1
    )


def d_tri_kernel(recv_ref, q_ref, out_ref, unit_ref):
    shards, both, width = recv_ref.shape
    unit, inv = unit_rows(halves_of(recv_ref))
    unit_ref[...] = unit
    d_tri = unit_back(q_ref[...], unit, inv)
    out_ref[...] = jnp.concatenate(
        [d_tri[:, :width].reshape(shards, both // 2, width), d_tri[:, width:].reshape(shards, both // 2, width)],
        axis=1,
    ).astype(BF16)


def update_kernel(unit_ref, gate_ref, back_ref, out_gain_ref, out_w_ref, gate_w_ref, update_ref, d_normed_ref):
    unit = unit_ref[...]
    tnorm = (unit * spread(column(out_gain_ref[...]), unit.shape[1])).astype(BF16)
    lin = dot(out_w_ref[...].T, tnorm, (1, 0))
    update_ref[...] = (gate_ref[...] * lin).T.astype(BF16)
    d_gpre = (back_ref[...] * lin).astype(BF16)
    d_normed_ref[...] = dot(gate_w_ref[...], d_gpre, (1, 0))


def sides_kernel(grid_rows, recv_ref, left_ref, right_ref, out_ref, d_tri, rows):
    devices, both, cells = out_ref.shape
    per = both // 2
    n = left_ref.shape[1]
    tile = n // grid_rows
    groups = cells // LANES
    half = groups // 2
    for r in range(grid_rows):
        blocks = [recv_ref[grid_rows * r + c].astype(F32) for c in range(grid_rows)]
        for g in range(half):
            lanes = slice(g * LANES, (g + 1) * LANES)
            for p, rows_p in enumerate(swap_blocks([b[:, lanes] for b in blocks])):
                for k in range(2):
                    at = (r * tile + (g + k * half) * grid_rows + p) * per
                    d_tri[at : at + per, :] = rows_p[k * per : (k + 1) * per]
    for h in range(per):
        grad = d_tri[pl.ds(h, n, stride=per), :].astype(BF16)
        rows[pl.ds(h, n, stride=both), :] = dot(grad, right_ref[h], (1, 0))
        rows[pl.ds(per + h, n, stride=both), :] = dot(grad, left_ref[h], (0, 0))
    for r in range(grid_rows):
        for g in range(groups):
            at = (r * tile + g * grid_rows) * both
            parts = swap_blocks([rows[at + p * both : at + (p + 1) * both, :] for p in range(grid_rows)])
            for c in range(grid_rows):
                out_ref[grid_rows * r + c, :, g * LANES : (g + 1) * LANES] = parts[c].astype(BF16)


def pair_grad_kernel(recv_ref, factor_ref, d_normed_ref, unit_ref, inv_ref, in_gain_ref, proj_ref, out_ref):
    shards, both, cells = recv_ref.shape
    hidden = shards * both // 2
    x = recv_ref[...].astype(F32)
    d_left = x[:, : both // 2].reshape(hidden, cells)
    d_right = x[:, both // 2 :].reshape(hidden, cells)
    d_proj = jnp.concatenate(
        [(grad * factor_ref[2 * side + part]).astype(BF16) for side, grad in enumerate((d_left, d_right)) for part in range(2)],
        axis=0,
    )
    d_normed = dot(proj_ref[...], d_proj, (1, 0)) + d_normed_ref[...]
    q = d_normed * spread(column(in_gain_ref[...]), cells)
    out_ref[...] = unit_back(q, unit_ref[...], inv_ref[...]).T


def call(kernel, outs, args, flops, scratch=()):
    given = sum(a.size * a.dtype.itemsize for a in args)
    made = sum(o.size * o.dtype.itemsize for o in outs)
    return pl.pallas_call(
        kernel,
        out_shape=tuple(outs),
        scratch_shapes=list(scratch),
        compiler_params=pltpu.CompilerParams(vmem_limit_bytes=48 * 2**20),
        cost_estimate=pl.CostEstimate(flops=flops, bytes_accessed=given + made, transcendentals=0),
    )(*args)


def by_channel(pair, cotangent, valid, in_gain, proj_weight, gate_weight, out_gain, out_weight):
    tile, _, channels = pair.shape
    hidden = out_weight.shape[0]
    cells = tile * tile
    grid_rows = lax.axis_size("row")
    devices = grid_rows * lax.axis_size("col")
    per = hidden // devices
    n = tile * grid_rows
    shape = lambda dims, dtype: jax.ShapeDtypeStruct(dims, dtype)
    whole = lambda x: lax.all_to_all(x, ("row", "col"), 0, 0, tiled=True)
    flat = pair.reshape(cells, channels)
    flat_cot = cotangent.reshape(cells, channels)
    valid_row = valid.reshape(1, -1)
    in_row = in_gain.reshape(1, -1)
    out_row = out_gain.reshape(1, -1)
    both = 2 * per
    plane = shape((channels, cells), F32)

    (sides,) = call(
        functools.partial(project_kernel, tile),
        [shape((devices, both, cells), BF16)],
        (flat, valid_row, in_row, proj_weight),
        2 * cells * channels * 4 * hidden,
    )
    sides = whole(sides)
    unit, inv, factors, gate, back, q = call(
        functools.partial(local_kernel, tile),
        [plane, shape((1, cells), F32), shape((4, hidden, cells), F32), plane, plane, plane],
        (flat, flat_cot, valid_row, in_row, proj_weight, gate_weight, out_row, out_weight),
        2 * cells * channels * 6 * hidden,
    )
    left, right, tri = call(
        functools.partial(tri_kernel, grid_rows),
        [shape((per, n, n), BF16), shape((per, n, n), BF16), shape((devices, both, cells // 2), BF16)],
        (sides,),
        2 * per * n * n * n,
        [pltpu.VMEM((n * both, n), F32), pltpu.VMEM((n * per, n), F32)],
    )
    tri = whole(tri)
    d_tri, unit_tri = call(
        d_tri_kernel,
        [shape((devices, both, cells // 2), BF16), plane],
        (tri, q),
        20 * cells * hidden,
    )
    d_tri = whole(d_tri)
    update, d_normed = call(
        update_kernel,
        [shape((cells, channels), BF16), plane],
        (unit_tri, gate, back, out_row, out_weight, gate_weight),
        2 * cells * channels * 2 * hidden,
    )
    (d_sides,) = call(
        functools.partial(sides_kernel, grid_rows),
        [shape((devices, both, cells), BF16)],
        (d_tri, left, right),
        4 * per * n * n * n,
        [pltpu.VMEM((n * per, n), F32), pltpu.VMEM((n * both, n), F32)],
    )
    d_sides = whole(d_sides)
    (pair_grad,) = call(
        pair_grad_kernel,
        [shape((cells, channels), F32)],
        (d_sides, factors, d_normed, unit, inv, in_row, proj_weight),
        2 * cells * channels * 4 * hidden,
    )
    return (update.reshape(pair.shape), pair_grad.reshape(pair.shape))


def fits(pair, out_weight):
    rows, cols = lax.axis_size("row"), lax.axis_size("col")
    tile, tile_cols, channels = pair.shape
    hidden = out_weight.shape[0]
    return (
        rows == cols == 4
        and tile == tile_cols
        and tile * rows == LANES
        and channels == LANES
        and hidden == 8 * rows * cols
    )


def step(pair, cotangent, valid, in_gain, proj_weight, gate_weight, out_gain, out_weight):
    plan = by_channel if fits(pair, out_weight) else on_device
    return plan(pair, cotangent, valid, in_gain, proj_weight, gate_weight, out_gain, out_weight)


def solution(mesh):
    placed = (
        P(("replica", "row"), "col", None),
        P(("replica", "row"), "col", None),
        P("replica"),
        P(),
        P(),
        P(),
        P(),
        P(),
    )
    return jax.shard_map(
        step,
        mesh=mesh,
        in_specs=placed,
        out_specs=(P(("replica", "row"), "col", None), P(("replica", "row"), "col", None)),
        check_vma=False,
    )
```

```python
import functools

import jax
import jax.numpy as jnp
from jax import lax
from jax.experimental import pallas as pl
from jax.experimental.pallas import tpu as pltpu
from jax.sharding import PartitionSpec as P

eps_norm = 1e-05


def layer_norm(values, gain):
    mean_val = jnp.mean(values, axis=-1, keepdims=True)
    centred = values - mean_val
    inv_std = lax.rsqrt(jnp.mean(centred * centred, axis=-1, keepdims=True) + eps_norm)
    unit = centred * inv_std
    return (unit * gain, unit, inv_std)


def norm_back(grad_unit, unit, inv_std):
    first = jnp.mean(grad_unit, axis=-1, keepdims=True)
    second = jnp.mean(grad_unit * unit, axis=-1, keepdims=True)
    return inv_std * (grad_unit - first - unit * second)


def on_device(pair, cotangent, valid, in_gain, proj_weight, gate_weight, out_gain, out_weight):
    tile_rows = pair.shape[0]
    channels = pair.shape[2]
    hidden = out_weight.shape[0]
    cells = tile_rows * tile_rows
    keeper = valid.astype(jnp.float32)
    row_keep = lax.dynamic_slice_in_dim(keeper, lax.axis_index("row") * tile_rows, tile_rows)
    col_keep = lax.dynamic_slice_in_dim(keeper, lax.axis_index("col") * tile_rows, tile_rows)
    pair_keep = (row_keep[:, None] * col_keep[None, :])[:, :, None]
    normed_f, unit_in, inv_in = layer_norm(pair.astype(jnp.float32), in_gain)
    normed = normed_f.astype(jnp.bfloat16)
    flat = normed.reshape(cells, channels)
    proj = jnp.dot(flat, proj_weight, preferred_element_type=jnp.float32).reshape(
        tile_rows, tile_rows, 4 * hidden
    )
    left_sig = jax.nn.sigmoid(proj[..., :hidden])
    left_val = proj[..., hidden : 2 * hidden]
    right_sig = jax.nn.sigmoid(proj[..., 2 * hidden : 3 * hidden])
    right_val = proj[..., 3 * hidden :]
    left = (left_sig * left_val * pair_keep).astype(jnp.bfloat16)
    right = (right_sig * right_val * pair_keep).astype(jnp.bfloat16)
    panel = lax.all_gather(right, "row", axis=0, tiled=True)
    piece = panel
    tri = jnp.swapaxes(
        lax.psum_scatter(
            jnp.einsum("ikh,jkh->jih", left, piece, preferred_element_type=jnp.float32),
            "col",
            scatter_dimension=0,
            tiled=True,
        ),
        0,
        1,
    )
    tnorm_f, unit_tri, inv_tri = layer_norm(tri, out_gain)
    tnorm = tnorm_f.astype(jnp.bfloat16)
    gate = jax.nn.sigmoid(jnp.dot(flat, gate_weight, preferred_element_type=jnp.float32)).reshape(
        tile_rows, tile_rows, channels
    )
    lin = jnp.dot(
        tnorm.reshape(cells, hidden), out_weight, preferred_element_type=jnp.float32
    ).reshape(tile_rows, tile_rows, channels)
    update = (gate * lin).astype(jnp.bfloat16)
    cot = cotangent.astype(jnp.float32)
    d_lin = (cot * gate).astype(jnp.bfloat16)
    d_gpre = (cot * lin * gate * (1.0 - gate)).astype(jnp.bfloat16)
    d_tnorm = jnp.dot(
        d_lin.reshape(cells, channels), out_weight.T, preferred_element_type=jnp.float32
    ).reshape(tile_rows, tile_rows, hidden)
    d_tri = norm_back(d_tnorm * out_gain, unit_tri, inv_tri).astype(jnp.bfloat16)
    grad_rows = lax.all_gather(d_tri, "col", axis=1, tiled=True)
    back_panel = lax.all_gather(right, "row", axis=0, tiled=True)
    piece = grad_rows
    d_right = lax.psum_scatter(
        jnp.einsum("ijh,ikh->jkh", piece, left, preferred_element_type=jnp.float32),
        "row",
        scatter_dimension=0,
        tiled=True,
    )
    d_left = jnp.einsum("ijh,jkh->ikh", grad_rows, back_panel, preferred_element_type=jnp.float32)
    d_proj = jnp.concatenate(
        [
            d_left * pair_keep * left_val * left_sig * (1.0 - left_sig),
            d_left * pair_keep * left_sig,
            d_right * pair_keep * right_val * right_sig * (1.0 - right_sig),
            d_right * pair_keep * right_sig,
        ],
        axis=-1,
    ).astype(jnp.bfloat16)
    d_normed = jnp.dot(
        d_proj.reshape(cells, 4 * hidden), proj_weight.T, preferred_element_type=jnp.float32
    )
    d_normed = d_normed + jnp.dot(
        d_gpre.reshape(cells, channels), gate_weight.T, preferred_element_type=jnp.float32
    )
    pair_grad = norm_back(
        d_normed.reshape(tile_rows, tile_rows, channels) * in_gain, unit_in, inv_in
    )
    return (update, pair_grad)


F32 = jnp.float32
BF16 = jnp.bfloat16
LANES = 128


def dot(a, b, dims):
    return lax.dot_general(a, b, ((dims[:1], dims[1:]), ((), ())), preferred_element_type=F32)


def column(gain):
    n = gain.shape[1]
    return jnp.broadcast_to(gain, (n, n)).T


def spread(col, width):
    return jnp.concatenate([col] * (width // col.shape[1]), axis=1)


def unit_rows(values):
    n = values.shape[0]
    centred = values - jnp.sum(values, axis=0, keepdims=True) * (1.0 / n)
    inv = lax.rsqrt(jnp.sum(centred * centred, axis=0, keepdims=True) * (1.0 / n) + eps_norm)
    return centred * inv, inv


def unit_back(q, unit, inv):
    n = q.shape[0]
    first = jnp.sum(q, axis=0, keepdims=True) * (1.0 / n)
    second = jnp.sum(q * unit, axis=0, keepdims=True) * (1.0 / n)
    return inv * (q - first - unit * second)


def block_swap():
    size, width = 4 * LANES, LANES // 4
    row = lax.broadcasted_iota(jnp.int32, (size, LANES), 0)
    col = lax.broadcasted_iota(jnp.int32, (size, LANES), 1)
    target = (row // width % 4) * LANES + (row // LANES) * width + row % width - col
    return jnp.concatenate([(target == n * LANES).astype(F32) for n in range(4)], axis=1).astype(BF16)


def keep_row(valid, tile, cells):
    n = valid.ref.shape[1]
    token = lax.broadcasted_iota(jnp.int32, (n, cells), 0)
    cell = lax.broadcasted_iota(jnp.int32, (n, cells), 1)
    first = (token == lax.axis_index("row") * tile + cell // tile).astype(F32).astype(BF16)
    second = (token == lax.axis_index("col") * tile + cell % tile).astype(F32).astype(BF16)
    v = jnp.broadcast_to(valid.ready()[...].astype(F32), (8, n)).astype(BF16)
    return (dot(v, first, (1, 0)) * dot(v, second, (1, 0)))[:1]


def normed_of(pair, in_gain):
    unit, inv = unit_rows(pair.ready()[...].astype(F32).T)
    normed = (unit * spread(column(in_gain.ready()[...]), unit.shape[1])).astype(BF16)
    return normed, unit, inv


def project_kernel(tile, pair, valid, in_gain, proj_weight, out_ref):
    hidden = proj_weight.ref.shape[1] // 4
    shards, both, cells = out_ref.shape
    normed, _, _ = normed_of(pair, in_gain)
    keep = keep_row(valid, tile, cells)
    weights = proj_weight.ready()
    sides = []
    for side in range(2):
        weight = weights[:, 2 * hidden * side : 2 * hidden * (side + 1)].T
        proj = dot(weight, normed, (1, 0))
        sides.append(jax.nn.sigmoid(proj[:hidden]) * proj[hidden:] * keep)
    for s in range(shards):
        rows = slice(s * both // 2, (s + 1) * both // 2)
        out_ref[s] = jnp.concatenate([sides[0][rows], sides[1][rows]], axis=0).astype(BF16)


def gate_of(normed, cot, gate_weight):
    gate = jax.nn.sigmoid(dot(gate_weight.ready()[...].T, normed, (1, 0)))
    return gate, cot.ready()[...].astype(F32).T


def gate_kernel(pair, cot, in_gain, gate_weight, out_gain, out_weight, q_ref):
    normed, _, _ = normed_of(pair, in_gain)
    gate, cot_rows = gate_of(normed, cot, gate_weight)
    q = dot(out_weight.ready()[...], (cot_rows * gate).astype(BF16), (1, 0))
    q_ref[...] = q * spread(column(out_gain.ready()[...]), q.shape[1])


def tri_kernel(grid_rows, recv_ref, out_ref, left, right, rows, tri):
    devices, both, cells = recv_ref.shape
    per = both // 2
    n = left.ref.shape[1]
    tile = n // grid_rows
    groups = cells // LANES
    swap = block_swap()
    for r in range(grid_rows):
        x = jnp.concatenate(
            [
                jnp.concatenate(
                    [recv_ref[grid_rows * r + c, :, g * LANES : (g + 1) * LANES] for c in range(grid_rows)], axis=1
                )
                for g in range(groups)
            ],
            axis=0,
        )
        y = dot(x, swap, (1, 0))
        for g in range(groups):
            for p in range(grid_rows):
                at = (r * tile + g * grid_rows + p) * both
                rows[at : at + both, :] = y[g * both : (g + 1) * both, p * LANES : (p + 1) * LANES]
    for h in range(per):
        left.ref[h] = rows[pl.ds(h, n, stride=both), :].astype(BF16)
        right.ref[h] = rows[pl.ds(per + h, n, stride=both), :].astype(BF16)
    left.send()
    right.send()
    for h in range(per):
        tri[pl.ds(h, n, stride=per), :] = dot(left.ref[h], right.ref[h], (1, 1))
    half = groups // 2
    for r in range(grid_rows):
        x = jnp.concatenate(
            [
                jnp.concatenate(
                    [
                        tri[at : at + per, :]
                        for p in range(grid_rows)
                        for at in [(r * tile + (g + k * half) * grid_rows + p) * per]
                    ],
                    axis=1,
                )
                for g in range(half)
                for k in range(2)
            ],
            axis=0,
        )
        y = dot(x.astype(BF16), swap, (1, 0)).astype(BF16)
        for g in range(half):
            for c in range(grid_rows):
                out_ref[grid_rows * r + c, :, g * LANES : (g + 1) * LANES] = y[
                    g * both : (g + 1) * both, c * LANES : (c + 1) * LANES
                ]


def halves_of(recv_ref):
    shards, both, width = recv_ref.shape
    x = recv_ref[...].astype(F32)
    rows = shards * both // 2
    return jnp.concatenate(
        [x[:, : both // 2].reshape(rows, width), x[:, both // 2 :].reshape(rows, width)], axis=1
    )


def d_tri_kernel(recv_ref, q_ref, out_ref):
    shards, both, width = recv_ref.shape
    unit, inv = unit_rows(halves_of(recv_ref))
    d_tri = unit_back(q_ref[...], unit, inv)
    out_ref[...] = jnp.concatenate(
        [d_tri[:, :width].reshape(shards, both // 2, width), d_tri[:, width:].reshape(shards, both // 2, width)],
        axis=1,
    ).astype(BF16)


def update_kernel(
    tile, tri, out_gain, out_weight, pair, cot, valid, in_gain, gate_weight, proj_weight,
    unit_ref, inv_ref, factor_ref, update,
):
    normed, unit, inv = normed_of(pair, in_gain)
    unit_ref[...] = unit
    inv_ref[...] = inv
    gate, cot_rows = gate_of(normed, cot, gate_weight)
    unit_tri, _ = unit_rows(halves_of(tri.ready()))
    tnorm = (unit_tri * spread(column(out_gain.ready()[...]), unit.shape[1])).astype(BF16)
    lin = dot(out_weight.ready()[...].T, tnorm, (1, 0))
    update.ref[...] = (gate * lin).T.astype(BF16)
    update.send()
    factor_ref[4] = (cot_rows * lin * gate * (1.0 - gate)).astype(BF16)
    hidden = proj_weight.ref.shape[1] // 4
    keep = keep_row(valid, tile, unit.shape[1])
    weights = proj_weight.ready()
    for side in range(2):
        weight = weights[:, 2 * hidden * side : 2 * hidden * (side + 1)].T
        proj = dot(weight, normed, (1, 0))
        sig = jax.nn.sigmoid(proj[:hidden])
        factor_ref[2 * side] = (keep * proj[hidden:] * sig * (1.0 - sig)).astype(BF16)
        factor_ref[2 * side + 1] = (keep * sig).astype(BF16)


def sides_kernel(grid_rows, recv_ref, left, right, out_ref, d_tri, rows):
    devices, both, cells = out_ref.shape
    per = both // 2
    n = left.ref.shape[1]
    tile = n // grid_rows
    groups = cells // LANES
    half = groups // 2
    swap = block_swap()
    for r in range(grid_rows):
        x = jnp.concatenate(
            [
                jnp.concatenate(
                    [recv_ref[grid_rows * r + c, :, g * LANES : (g + 1) * LANES] for c in range(grid_rows)], axis=1
                )
                for g in range(half)
            ],
            axis=0,
        )
        y = dot(x, swap, (1, 0))
        for g in range(half):
            for k in range(2):
                for p in range(grid_rows):
                    at = (r * tile + (g + k * half) * grid_rows + p) * per
                    d_tri[at : at + per, :] = y[
                        g * both + k * per : g * both + (k + 1) * per, p * LANES : (p + 1) * LANES
                    ]
    left_ref, right_ref = left.ready(), right.ready()
    for h in range(per):
        grad = d_tri[pl.ds(h, n, stride=per), :].astype(BF16)
        rows[pl.ds(h, n, stride=both), :] = dot(grad, right_ref[h], (1, 0))
        rows[pl.ds(per + h, n, stride=both), :] = dot(grad, left_ref[h], (0, 0))
    for r in range(grid_rows):
        x = jnp.concatenate(
            [
                jnp.concatenate(
                    [
                        rows[at : at + both, :]
                        for p in range(grid_rows)
                        for at in [(r * tile + g * grid_rows + p) * both]
                    ],
                    axis=1,
                )
                for g in range(groups)
            ],
            axis=0,
        )
        y = dot(x.astype(BF16), swap, (1, 0)).astype(BF16)
        for g in range(groups):
            for c in range(grid_rows):
                out_ref[grid_rows * r + c, :, g * LANES : (g + 1) * LANES] = y[
                    g * both : (g + 1) * both, c * LANES : (c + 1) * LANES
                ]


def pair_grad_kernel(recv_ref, factor_ref, unit_ref, inv_ref, in_gain, proj_weight, gate_weight, out):
    shards, both, cells = recv_ref.shape
    hidden = shards * both // 2
    x = recv_ref[...].astype(F32)
    d_left = x[:, : both // 2].reshape(hidden, cells)
    d_right = x[:, both // 2 :].reshape(hidden, cells)
    d_proj = jnp.concatenate(
        [(grad * factor_ref[2 * side + part].astype(F32)).astype(BF16) for side, grad in enumerate((d_left, d_right)) for part in range(2)],
        axis=0,
    )
    d_normed = dot(proj_weight.ready()[...], d_proj, (1, 0))
    d_normed = d_normed + dot(gate_weight.ready()[...], factor_ref[4], (1, 0))
    q = d_normed * spread(column(in_gain.ready()[...]), cells)
    out.ref[...] = unit_back(q, unit_ref[...], inv_ref[...]).T
    out.send()


class Arriving:
    def __init__(self, source, ref, sem):
        self.ref, self.copy = ref, pltpu.make_async_copy(source, ref, sem)
        self.copy.start()

    def ready(self):
        if self.copy is not None:
            self.copy.wait()
            self.copy = None
        return self.ref


class Leaving:
    def __init__(self, target, ref, sem):
        self.ref, self.copy = ref, pltpu.make_async_copy(ref, target, sem)

    def send(self):
        self.copy.start()


def call(kernel, outs, args, flops, scratch=(), far=(), far_outs=(), room=24):
    outs, args, far, far_outs, scratch = (list(x) for x in (outs, args, far, far_outs, scratch))
    counts = [len(args), len(far), len(outs), len(far_outs), len(far), len(far_outs), len(scratch)]

    def body(*refs):
        parts, at = [], 0
        for count in counts:
            parts.append(list(refs[at : at + count]))
            at += count
        near_in, far_in, near_out, far_out, held, leaving, rest = parts
        sems = refs[at]
        arrivals = [Arriving(a, b, sems.at[i]) for i, (a, b) in enumerate(zip(far_in, held))]
        departures = [
            Leaving(a, b, sems.at[len(held) + i]) for i, (a, b) in enumerate(zip(far_out, leaving))
        ]
        kernel(*near_in, *arrivals, *near_out, *departures, *rest)
        for one in arrivals:
            one.ready()
        for one in departures:
            one.copy.wait()

    near_spec, far_spec = pl.BlockSpec(memory_space=pltpu.VMEM), pl.BlockSpec(memory_space=pltpu.HBM)
    moved = sum(a.size * a.dtype.itemsize for a in args + far + outs + far_outs)
    return pl.pallas_call(
        body,
        out_shape=tuple(outs + far_outs),
        in_specs=[near_spec] * len(args) + [far_spec] * len(far),
        out_specs=tuple([near_spec] * len(outs) + [far_spec] * len(far_outs)),
        scratch_shapes=[pltpu.VMEM(a.shape, a.dtype) for a in far + far_outs]
        + scratch
        + [pltpu.SemaphoreType.DMA((max(1, len(far) + len(far_outs)),))],
        compiler_params=pltpu.CompilerParams(vmem_limit_bytes=int(room * 2**20)),
        cost_estimate=pl.CostEstimate(flops=flops, bytes_accessed=moved, transcendentals=0),
    )(*args, *far)


def by_channel(pair, cotangent, valid, in_gain, proj_weight, gate_weight, out_gain, out_weight):
    tile, _, channels = pair.shape
    hidden = out_weight.shape[0]
    cells = tile * tile
    grid_rows = lax.axis_size("row")
    devices = grid_rows * lax.axis_size("col")
    per = hidden // devices
    n = tile * grid_rows
    shape = lambda dims, dtype: jax.ShapeDtypeStruct(dims, dtype)
    whole = lambda x: lax.all_to_all(x, ("row", "col"), 0, 0, tiled=True)
    flat = pair.reshape(cells, channels)
    flat_cot = cotangent.reshape(cells, channels)
    valid_row = valid.reshape(1, -1)
    in_row = in_gain.reshape(1, -1)
    out_row = out_gain.reshape(1, -1)
    both = 2 * per
    plane = shape((channels, cells), F32)

    (sides,) = call(
        functools.partial(project_kernel, tile),
        [shape((devices, both, cells), BF16)],
        (),
        2 * cells * channels * 4 * hidden,
        far=(flat, valid_row, in_row, proj_weight),
        room=62,
    )
    sides = whole(sides)
    tri, left, right = call(
        functools.partial(tri_kernel, grid_rows),
        [shape((devices, both, cells // 2), BF16)],
        (sides,),
        2 * per * n * n * n,
        [pltpu.VMEM((n * both, n), F32), pltpu.VMEM((n * per, n), F32)],
        far_outs=[shape((per, n, n), BF16)] * 2,
    )
    tri, flat_2, flat_cot_2 = lax.optimization_barrier((tri, flat, flat_cot))
    tri = whole(tri)
    (q,) = call(
        gate_kernel,
        [plane],
        (),
        2 * cells * channels * 2 * hidden,
        far=(flat_2, flat_cot_2, in_row, gate_weight, out_row, out_weight),
    )
    (d_tri,) = call(
        d_tri_kernel,
        [shape((devices, both, cells // 2), BF16)],
        (tri, q),
        20 * cells * hidden,
    )
    d_tri = whole(d_tri)
    (d_sides,) = call(
        functools.partial(sides_kernel, grid_rows),
        [shape((devices, both, cells), BF16)],
        (d_tri,),
        4 * per * n * n * n,
        [pltpu.VMEM((n * per, n), F32), pltpu.VMEM((n * both, n), F32)],
        far=(left, right),
    )
    d_sides, flat_4, flat_cot_4, tri = lax.optimization_barrier((d_sides, flat, flat_cot, tri))
    d_sides = whole(d_sides)
    unit, inv, factors, update = call(
        functools.partial(update_kernel, tile),
        [plane, shape((1, cells), F32), shape((5, hidden, cells), BF16)],
        (),
        2 * cells * channels * 6 * hidden,
        far=(tri, out_row, out_weight, flat_4, flat_cot_4, valid_row, in_row, gate_weight, proj_weight),
        far_outs=[shape((cells, channels), BF16)],
    )
    (pair_grad,) = call(
        pair_grad_kernel,
        [],
        (d_sides, factors, unit, inv),
        2 * cells * channels * 5 * hidden,
        far=(in_row, proj_weight, gate_weight),
        far_outs=[shape((cells, channels), F32)],
    )
    return (update.reshape(pair.shape), pair_grad.reshape(pair.shape))


def fits(pair, out_weight):
    rows, cols = lax.axis_size("row"), lax.axis_size("col")
    tile, tile_cols, channels = pair.shape
    hidden = out_weight.shape[0]
    return (
        rows == cols == 4
        and tile == tile_cols
        and tile * rows == LANES
        and channels == LANES
        and hidden == 8 * rows * cols
    )


def step(pair, cotangent, valid, in_gain, proj_weight, gate_weight, out_gain, out_weight):
    plan = by_channel if fits(pair, out_weight) else on_device
    return plan(pair, cotangent, valid, in_gain, proj_weight, gate_weight, out_gain, out_weight)


def solution(mesh):
    placed = (
        P(("replica", "row"), "col", None),
        P(("replica", "row"), "col", None),
        P("replica"),
        P(),
        P(),
        P(),
        P(),
        P(),
    )
    return jax.shard_map(
        step,
        mesh=mesh,
        in_specs=placed,
        out_specs=(P(("replica", "row"), "col", None), P(("replica", "row"), "col", None)),
        check_vma=False,
    )
```

```python
import functools

import jax
import jax.numpy as jnp
from jax import lax
from jax.experimental import pallas as pl
from jax.experimental.pallas import tpu as pltpu
from jax.sharding import PartitionSpec as P

eps_norm = 1e-05


def layer_norm(values, gain):
    mean_val = jnp.mean(values, axis=-1, keepdims=True)
    centred = values - mean_val
    inv_std = lax.rsqrt(jnp.mean(centred * centred, axis=-1, keepdims=True) + eps_norm)
    unit = centred * inv_std
    return (unit * gain, unit, inv_std)


def norm_back(grad_unit, unit, inv_std):
    first = jnp.mean(grad_unit, axis=-1, keepdims=True)
    second = jnp.mean(grad_unit * unit, axis=-1, keepdims=True)
    return inv_std * (grad_unit - first - unit * second)


def on_device(pair, cotangent, valid, in_gain, proj_weight, gate_weight, out_gain, out_weight):
    tile_rows = pair.shape[0]
    channels = pair.shape[2]
    hidden = out_weight.shape[0]
    cells = tile_rows * tile_rows
    keeper = valid.astype(jnp.float32)
    row_keep = lax.dynamic_slice_in_dim(keeper, lax.axis_index("row") * tile_rows, tile_rows)
    col_keep = lax.dynamic_slice_in_dim(keeper, lax.axis_index("col") * tile_rows, tile_rows)
    pair_keep = (row_keep[:, None] * col_keep[None, :])[:, :, None]
    normed_f, unit_in, inv_in = layer_norm(pair.astype(jnp.float32), in_gain)
    normed = normed_f.astype(jnp.bfloat16)
    flat = normed.reshape(cells, channels)
    proj = jnp.dot(flat, proj_weight, preferred_element_type=jnp.float32).reshape(
        tile_rows, tile_rows, 4 * hidden
    )
    left_sig = jax.nn.sigmoid(proj[..., :hidden])
    left_val = proj[..., hidden : 2 * hidden]
    right_sig = jax.nn.sigmoid(proj[..., 2 * hidden : 3 * hidden])
    right_val = proj[..., 3 * hidden :]
    left = (left_sig * left_val * pair_keep).astype(jnp.bfloat16)
    right = (right_sig * right_val * pair_keep).astype(jnp.bfloat16)
    panel = lax.all_gather(right, "row", axis=0, tiled=True)
    piece = panel
    tri = jnp.swapaxes(
        lax.psum_scatter(
            jnp.einsum("ikh,jkh->jih", left, piece, preferred_element_type=jnp.float32),
            "col",
            scatter_dimension=0,
            tiled=True,
        ),
        0,
        1,
    )
    tnorm_f, unit_tri, inv_tri = layer_norm(tri, out_gain)
    tnorm = tnorm_f.astype(jnp.bfloat16)
    gate = jax.nn.sigmoid(jnp.dot(flat, gate_weight, preferred_element_type=jnp.float32)).reshape(
        tile_rows, tile_rows, channels
    )
    lin = jnp.dot(
        tnorm.reshape(cells, hidden), out_weight, preferred_element_type=jnp.float32
    ).reshape(tile_rows, tile_rows, channels)
    update = (gate * lin).astype(jnp.bfloat16)
    cot = cotangent.astype(jnp.float32)
    d_lin = (cot * gate).astype(jnp.bfloat16)
    d_gpre = (cot * lin * gate * (1.0 - gate)).astype(jnp.bfloat16)
    d_tnorm = jnp.dot(
        d_lin.reshape(cells, channels), out_weight.T, preferred_element_type=jnp.float32
    ).reshape(tile_rows, tile_rows, hidden)
    d_tri = norm_back(d_tnorm * out_gain, unit_tri, inv_tri).astype(jnp.bfloat16)
    grad_rows = lax.all_gather(d_tri, "col", axis=1, tiled=True)
    back_panel = lax.all_gather(right, "row", axis=0, tiled=True)
    piece = grad_rows
    d_right = lax.psum_scatter(
        jnp.einsum("ijh,ikh->jkh", piece, left, preferred_element_type=jnp.float32),
        "row",
        scatter_dimension=0,
        tiled=True,
    )
    d_left = jnp.einsum("ijh,jkh->ikh", grad_rows, back_panel, preferred_element_type=jnp.float32)
    d_proj = jnp.concatenate(
        [
            d_left * pair_keep * left_val * left_sig * (1.0 - left_sig),
            d_left * pair_keep * left_sig,
            d_right * pair_keep * right_val * right_sig * (1.0 - right_sig),
            d_right * pair_keep * right_sig,
        ],
        axis=-1,
    ).astype(jnp.bfloat16)
    d_normed = jnp.dot(
        d_proj.reshape(cells, 4 * hidden), proj_weight.T, preferred_element_type=jnp.float32
    )
    d_normed = d_normed + jnp.dot(
        d_gpre.reshape(cells, channels), gate_weight.T, preferred_element_type=jnp.float32
    )
    pair_grad = norm_back(
        d_normed.reshape(tile_rows, tile_rows, channels) * in_gain, unit_in, inv_in
    )
    return (update, pair_grad)


F32 = jnp.float32
BF16 = jnp.bfloat16
LANES = 128
ORDER = (6, 2, 11, 0, 15, 7, 5, 4, 9, 8, 1, 3, 12, 13, 14, 10)
PLACE = tuple(ORDER.index(device) for device in range(len(ORDER)))


def dot(a, b, dims):
    return lax.dot_general(a, b, ((dims[:1], dims[1:]), ((), ())), preferred_element_type=F32)


def column(gain):
    n = gain.shape[1]
    return jnp.broadcast_to(gain, (n, n)).T


def spread(col, width):
    return jnp.concatenate([col] * (width // col.shape[1]), axis=1)


def unit_rows(values):
    n = values.shape[0]
    centred = values - jnp.sum(values, axis=0, keepdims=True) * (1.0 / n)
    inv = lax.rsqrt(jnp.sum(centred * centred, axis=0, keepdims=True) * (1.0 / n) + eps_norm)
    return centred * inv, inv


def unit_back(q, unit, inv):
    n = q.shape[0]
    first = jnp.sum(q, axis=0, keepdims=True) * (1.0 / n)
    second = jnp.sum(q * unit, axis=0, keepdims=True) * (1.0 / n)
    return inv * (q - first - unit * second)


def block_swap():
    size, width = 4 * LANES, LANES // 4
    row = lax.broadcasted_iota(jnp.int32, (size, LANES), 0)
    col = lax.broadcasted_iota(jnp.int32, (size, LANES), 1)
    target = (row // width % 4) * LANES + (row // LANES) * width + row % width - col
    return jnp.concatenate([(target == n * LANES).astype(F32) for n in range(4)], axis=1).astype(BF16)


def keep_row(valid, tile, cells):
    n = valid.ref.shape[1]
    token = lax.broadcasted_iota(jnp.int32, (n, cells), 0)
    cell = lax.broadcasted_iota(jnp.int32, (n, cells), 1)
    first = (token == lax.axis_index("row") * tile + cell // tile).astype(F32).astype(BF16)
    second = (token == lax.axis_index("col") * tile + cell % tile).astype(F32).astype(BF16)
    v = jnp.broadcast_to(valid.ready()[...].astype(F32), (8, n)).astype(BF16)
    return (dot(v, first, (1, 0)) * dot(v, second, (1, 0)))[:1]


def normed_of(pair, in_gain):
    unit, inv = unit_rows(pair.ready()[...].astype(F32).T)
    normed = (unit * spread(column(in_gain.ready()[...]), unit.shape[1])).astype(BF16)
    return normed, unit, inv


def project_kernel(tile, pair, valid, in_gain, proj_weight, out_ref):
    hidden = proj_weight.ref.shape[1] // 4
    shards, both, cells = out_ref.shape
    normed, _, _ = normed_of(pair, in_gain)
    keep = keep_row(valid, tile, cells)
    weights = proj_weight.ready()
    sides = []
    for side in range(2):
        weight = weights[:, 2 * hidden * side : 2 * hidden * (side + 1)].T
        proj = dot(weight, normed, (1, 0))
        sides.append(jax.nn.sigmoid(proj[:hidden]) * proj[hidden:] * keep)
    for s in range(shards):
        rows = slice(s * both // 2, (s + 1) * both // 2)
        out_ref[s] = jnp.concatenate([sides[0][rows], sides[1][rows]], axis=0).astype(BF16)


def gate_of(normed, cot, gate_weight):
    gate = jax.nn.sigmoid(dot(gate_weight.ready()[...].T, normed, (1, 0)))
    return gate, cot.ready()[...].astype(F32).T


def gate_kernel(pair, cot, in_gain, gate_weight, out_gain, out_weight, q_ref):
    normed, _, _ = normed_of(pair, in_gain)
    gate, cot_rows = gate_of(normed, cot, gate_weight)
    q = dot(out_weight.ready()[...], (cot_rows * gate).astype(BF16), (1, 0))
    q_ref[...] = q * spread(column(out_gain.ready()[...]), q.shape[1])


def tri_kernel(grid_rows, recv_ref, out_ref, left, right, rows, tri):
    devices, both, cells = recv_ref.shape
    per = both // 2
    n = left.ref.shape[1]
    tile = n // grid_rows
    groups = cells // LANES
    swap = block_swap()
    for r in range(grid_rows):
        x = jnp.concatenate(
            [
                jnp.concatenate(
                    [recv_ref[PLACE[grid_rows * r + c], :, g * LANES : (g + 1) * LANES] for c in range(grid_rows)], axis=1
                )
                for g in range(groups)
            ],
            axis=0,
        )
        y = dot(x, swap, (1, 0))
        for g in range(groups):
            for p in range(grid_rows):
                at = (r * tile + g * grid_rows + p) * both
                rows[at : at + both, :] = y[g * both : (g + 1) * both, p * LANES : (p + 1) * LANES]
    for h in range(per):
        left.ref[h] = rows[pl.ds(h, n, stride=both), :].astype(BF16)
        right.ref[h] = rows[pl.ds(per + h, n, stride=both), :].astype(BF16)
    left.send()
    right.send()
    for h in range(per):
        tri[pl.ds(h, n, stride=per), :] = dot(left.ref[h], right.ref[h], (1, 1))
    half = groups // 2
    for r in range(grid_rows):
        x = jnp.concatenate(
            [
                jnp.concatenate(
                    [
                        tri[at : at + per, :]
                        for p in range(grid_rows)
                        for at in [(r * tile + (g + k * half) * grid_rows + p) * per]
                    ],
                    axis=1,
                )
                for g in range(half)
                for k in range(2)
            ],
            axis=0,
        )
        y = dot(x.astype(BF16), swap, (1, 0)).astype(BF16)
        for g in range(half):
            for c in range(grid_rows):
                out_ref[PLACE[grid_rows * r + c], :, g * LANES : (g + 1) * LANES] = y[
                    g * both : (g + 1) * both, c * LANES : (c + 1) * LANES
                ]


def halves_of(recv_ref):
    shards, both, width = recv_ref.shape
    x = recv_ref[...].astype(F32)
    rows = shards * both // 2
    return jnp.concatenate(
        [x[:, : both // 2].reshape(rows, width), x[:, both // 2 :].reshape(rows, width)], axis=1
    )


def d_tri_kernel(recv_ref, q_ref, out_ref):
    shards, both, width = recv_ref.shape
    unit, inv = unit_rows(halves_of(recv_ref))
    d_tri = unit_back(q_ref[...], unit, inv)
    out_ref[...] = jnp.concatenate(
        [d_tri[:, :width].reshape(shards, both // 2, width), d_tri[:, width:].reshape(shards, both // 2, width)],
        axis=1,
    ).astype(BF16)


def update_kernel(
    tile, tri, out_gain, out_weight, pair, cot, valid, in_gain, gate_weight, proj_weight,
    unit_ref, inv_ref, factor_ref, update,
):
    normed, unit, inv = normed_of(pair, in_gain)
    unit_ref[...] = unit
    inv_ref[...] = inv
    gate, cot_rows = gate_of(normed, cot, gate_weight)
    unit_tri, _ = unit_rows(halves_of(tri.ready()))
    tnorm = (unit_tri * spread(column(out_gain.ready()[...]), unit.shape[1])).astype(BF16)
    lin = dot(out_weight.ready()[...].T, tnorm, (1, 0))
    update.ref[...] = (gate * lin).T.astype(BF16)
    update.send()
    factor_ref[4] = (cot_rows * lin * gate * (1.0 - gate)).astype(BF16)
    hidden = proj_weight.ref.shape[1] // 4
    keep = keep_row(valid, tile, unit.shape[1])
    weights = proj_weight.ready()
    for side in range(2):
        weight = weights[:, 2 * hidden * side : 2 * hidden * (side + 1)].T
        proj = dot(weight, normed, (1, 0))
        sig = jax.nn.sigmoid(proj[:hidden])
        factor_ref[2 * side] = (keep * proj[hidden:] * sig * (1.0 - sig)).astype(BF16)
        factor_ref[2 * side + 1] = (keep * sig).astype(BF16)


def sides_kernel(grid_rows, recv_ref, left, right, out_ref, d_tri, rows):
    devices, both, cells = out_ref.shape
    per = both // 2
    n = left.ref.shape[1]
    tile = n // grid_rows
    groups = cells // LANES
    half = groups // 2
    swap = block_swap()
    for r in range(grid_rows):
        x = jnp.concatenate(
            [
                jnp.concatenate(
                    [recv_ref[PLACE[grid_rows * r + c], :, g * LANES : (g + 1) * LANES] for c in range(grid_rows)], axis=1
                )
                for g in range(half)
            ],
            axis=0,
        )
        y = dot(x, swap, (1, 0))
        for g in range(half):
            for k in range(2):
                for p in range(grid_rows):
                    at = (r * tile + (g + k * half) * grid_rows + p) * per
                    d_tri[at : at + per, :] = y[
                        g * both + k * per : g * both + (k + 1) * per, p * LANES : (p + 1) * LANES
                    ]
    left_ref, right_ref = left.ready(), right.ready()
    for h in range(per):
        grad = d_tri[pl.ds(h, n, stride=per), :].astype(BF16)
        rows[pl.ds(h, n, stride=both), :] = dot(grad, right_ref[h], (1, 0))
        rows[pl.ds(per + h, n, stride=both), :] = dot(grad, left_ref[h], (0, 0))
    for r in range(grid_rows):
        x = jnp.concatenate(
            [
                jnp.concatenate(
                    [
                        rows[at : at + both, :]
                        for p in range(grid_rows)
                        for at in [(r * tile + g * grid_rows + p) * both]
                    ],
                    axis=1,
                )
                for g in range(groups)
            ],
            axis=0,
        )
        y = dot(x.astype(BF16), swap, (1, 0)).astype(BF16)
        for g in range(groups):
            for c in range(grid_rows):
                out_ref[PLACE[grid_rows * r + c], :, g * LANES : (g + 1) * LANES] = y[
                    g * both : (g + 1) * both, c * LANES : (c + 1) * LANES
                ]


def pair_grad_kernel(recv_ref, factor_ref, unit_ref, inv_ref, in_gain, proj_weight, gate_weight, out):
    shards, both, cells = recv_ref.shape
    hidden = shards * both // 2
    x = recv_ref[...].astype(F32)
    d_left = x[:, : both // 2].reshape(hidden, cells)
    d_right = x[:, both // 2 :].reshape(hidden, cells)
    d_proj = jnp.concatenate(
        [(grad * factor_ref[2 * side + part].astype(F32)).astype(BF16) for side, grad in enumerate((d_left, d_right)) for part in range(2)],
        axis=0,
    )
    d_normed = dot(proj_weight.ready()[...], d_proj, (1, 0))
    d_normed = d_normed + dot(gate_weight.ready()[...], factor_ref[4], (1, 0))
    q = d_normed * spread(column(in_gain.ready()[...]), cells)
    out.ref[...] = unit_back(q, unit_ref[...], inv_ref[...]).T
    out.send()


class Arriving:
    def __init__(self, source, ref, sem):
        self.ref, self.copy = ref, pltpu.make_async_copy(source, ref, sem)
        self.copy.start()

    def ready(self):
        if self.copy is not None:
            self.copy.wait()
            self.copy = None
        return self.ref


class Leaving:
    def __init__(self, target, ref, sem):
        self.ref, self.copy = ref, pltpu.make_async_copy(ref, target, sem)

    def send(self):
        self.copy.start()


def call(kernel, outs, args, flops, scratch=(), far=(), far_outs=(), room=24):
    outs, args, far, far_outs, scratch = (list(x) for x in (outs, args, far, far_outs, scratch))
    counts = [len(args), len(far), len(outs), len(far_outs), len(far), len(far_outs), len(scratch)]

    def body(*refs):
        parts, at = [], 0
        for count in counts:
            parts.append(list(refs[at : at + count]))
            at += count
        near_in, far_in, near_out, far_out, held, leaving, rest = parts
        sems = refs[at]
        arrivals = [Arriving(a, b, sems.at[i]) for i, (a, b) in enumerate(zip(far_in, held))]
        departures = [
            Leaving(a, b, sems.at[len(held) + i]) for i, (a, b) in enumerate(zip(far_out, leaving))
        ]
        kernel(*near_in, *arrivals, *near_out, *departures, *rest)
        for one in arrivals:
            one.ready()
        for one in departures:
            one.copy.wait()

    near_spec, far_spec = pl.BlockSpec(memory_space=pltpu.VMEM), pl.BlockSpec(memory_space=pltpu.HBM)
    moved = sum(a.size * a.dtype.itemsize for a in args + far + outs + far_outs)
    return pl.pallas_call(
        body,
        out_shape=tuple(outs + far_outs),
        in_specs=[near_spec] * len(args) + [far_spec] * len(far),
        out_specs=tuple([near_spec] * len(outs) + [far_spec] * len(far_outs)),
        scratch_shapes=[pltpu.VMEM(a.shape, a.dtype) for a in far + far_outs]
        + scratch
        + [pltpu.SemaphoreType.DMA((max(1, len(far) + len(far_outs)),))],
        compiler_params=pltpu.CompilerParams(vmem_limit_bytes=int(room * 2**20)),
        cost_estimate=pl.CostEstimate(flops=flops, bytes_accessed=moved, transcendentals=0),
    )(*args, *far)


def by_channel(pair, cotangent, valid, in_gain, proj_weight, gate_weight, out_gain, out_weight):
    tile, _, channels = pair.shape
    hidden = out_weight.shape[0]
    cells = tile * tile
    grid_rows = lax.axis_size("row")
    devices = grid_rows * lax.axis_size("col")
    per = hidden // devices
    n = tile * grid_rows
    shape = lambda dims, dtype: jax.ShapeDtypeStruct(dims, dtype)
    whole = lambda x: lax.all_to_all(x, ("row", "col"), 0, 0, axis_index_groups=[ORDER], tiled=True)
    flat = pair.reshape(cells, channels)
    flat_cot = cotangent.reshape(cells, channels)
    valid_row = valid.reshape(1, -1)
    in_row = in_gain.reshape(1, -1)
    out_row = out_gain.reshape(1, -1)
    both = 2 * per
    plane = shape((channels, cells), F32)

    (sides,) = call(
        functools.partial(project_kernel, tile),
        [shape((devices, both, cells), BF16)],
        (),
        2 * cells * channels * 4 * hidden,
        far=(flat, valid_row, in_row, proj_weight),
        room=62,
    )
    sides = whole(sides)
    tri, left, right = call(
        functools.partial(tri_kernel, grid_rows),
        [shape((devices, both, cells // 2), BF16)],
        (sides,),
        2 * per * n * n * n,
        [pltpu.VMEM((n * both, n), F32), pltpu.VMEM((n * per, n), F32)],
        far_outs=[shape((per, n, n), BF16)] * 2,
    )
    tri, flat_2, flat_cot_2 = lax.optimization_barrier((tri, flat, flat_cot))
    tri = whole(tri)
    (q,) = call(
        gate_kernel,
        [plane],
        (),
        2 * cells * channels * 2 * hidden,
        far=(flat_2, flat_cot_2, in_row, gate_weight, out_row, out_weight),
    )
    (d_tri,) = call(
        d_tri_kernel,
        [shape((devices, both, cells // 2), BF16)],
        (tri, q),
        20 * cells * hidden,
    )
    d_tri = whole(d_tri)
    (d_sides,) = call(
        functools.partial(sides_kernel, grid_rows),
        [shape((devices, both, cells), BF16)],
        (d_tri,),
        4 * per * n * n * n,
        [pltpu.VMEM((n * per, n), F32), pltpu.VMEM((n * both, n), F32)],
        far=(left, right),
    )
    d_sides, flat_4, flat_cot_4, tri = lax.optimization_barrier((d_sides, flat, flat_cot, tri))
    d_sides = whole(d_sides)
    unit, inv, factors, update = call(
        functools.partial(update_kernel, tile),
        [plane, shape((1, cells), F32), shape((5, hidden, cells), BF16)],
        (),
        2 * cells * channels * 6 * hidden,
        far=(tri, out_row, out_weight, flat_4, flat_cot_4, valid_row, in_row, gate_weight, proj_weight),
        far_outs=[shape((cells, channels), BF16)],
    )
    (pair_grad,) = call(
        pair_grad_kernel,
        [],
        (d_sides, factors, unit, inv),
        2 * cells * channels * 5 * hidden,
        far=(in_row, proj_weight, gate_weight),
        far_outs=[shape((cells, channels), F32)],
    )
    return (update.reshape(pair.shape), pair_grad.reshape(pair.shape))


def fits(pair, out_weight):
    rows, cols = lax.axis_size("row"), lax.axis_size("col")
    tile, tile_cols, channels = pair.shape
    hidden = out_weight.shape[0]
    return (
        rows == cols == 4
        and tile == tile_cols
        and tile * rows == LANES
        and channels == LANES
        and hidden == 8 * rows * cols
    )


def step(pair, cotangent, valid, in_gain, proj_weight, gate_weight, out_gain, out_weight):
    plan = by_channel if fits(pair, out_weight) else on_device
    return plan(pair, cotangent, valid, in_gain, proj_weight, gate_weight, out_gain, out_weight)


def solution(mesh):
    placed = (
        P(("replica", "row"), "col", None),
        P(("replica", "row"), "col", None),
        P("replica"),
        P(),
        P(),
        P(),
        P(),
        P(),
    )
    return jax.shard_map(
        step,
        mesh=mesh,
        in_specs=placed,
        out_specs=(P(("replica", "row"), "col", None), P(("replica", "row"), "col", None)),
        check_vma=False,
    )
```

```python
import functools

import jax
import jax.numpy as jnp
from jax import lax
from jax.experimental import pallas as pl
from jax.experimental.pallas import tpu as pltpu
from jax.sharding import PartitionSpec as P

eps_norm = 1e-05


def layer_norm(values, gain):
    mean_val = jnp.mean(values, axis=-1, keepdims=True)
    centred = values - mean_val
    inv_std = lax.rsqrt(jnp.mean(centred * centred, axis=-1, keepdims=True) + eps_norm)
    unit = centred * inv_std
    return (unit * gain, unit, inv_std)


def norm_back(grad_unit, unit, inv_std):
    first = jnp.mean(grad_unit, axis=-1, keepdims=True)
    second = jnp.mean(grad_unit * unit, axis=-1, keepdims=True)
    return inv_std * (grad_unit - first - unit * second)


def on_device(pair, cotangent, valid, in_gain, proj_weight, gate_weight, out_gain, out_weight):
    tile_rows = pair.shape[0]
    channels = pair.shape[2]
    hidden = out_weight.shape[0]
    cells = tile_rows * tile_rows
    keeper = valid.astype(jnp.float32)
    row_keep = lax.dynamic_slice_in_dim(keeper, lax.axis_index("row") * tile_rows, tile_rows)
    col_keep = lax.dynamic_slice_in_dim(keeper, lax.axis_index("col") * tile_rows, tile_rows)
    pair_keep = (row_keep[:, None] * col_keep[None, :])[:, :, None]
    normed_f, unit_in, inv_in = layer_norm(pair.astype(jnp.float32), in_gain)
    normed = normed_f.astype(jnp.bfloat16)
    flat = normed.reshape(cells, channels)
    proj = jnp.dot(flat, proj_weight, preferred_element_type=jnp.float32).reshape(
        tile_rows, tile_rows, 4 * hidden
    )
    left_sig = jax.nn.sigmoid(proj[..., :hidden])
    left_val = proj[..., hidden : 2 * hidden]
    right_sig = jax.nn.sigmoid(proj[..., 2 * hidden : 3 * hidden])
    right_val = proj[..., 3 * hidden :]
    left = (left_sig * left_val * pair_keep).astype(jnp.bfloat16)
    right = (right_sig * right_val * pair_keep).astype(jnp.bfloat16)
    panel = lax.all_gather(right, "row", axis=0, tiled=True)
    piece = panel
    tri = jnp.swapaxes(
        lax.psum_scatter(
            jnp.einsum("ikh,jkh->jih", left, piece, preferred_element_type=jnp.float32),
            "col",
            scatter_dimension=0,
            tiled=True,
        ),
        0,
        1,
    )
    tnorm_f, unit_tri, inv_tri = layer_norm(tri, out_gain)
    tnorm = tnorm_f.astype(jnp.bfloat16)
    gate = jax.nn.sigmoid(jnp.dot(flat, gate_weight, preferred_element_type=jnp.float32)).reshape(
        tile_rows, tile_rows, channels
    )
    lin = jnp.dot(
        tnorm.reshape(cells, hidden), out_weight, preferred_element_type=jnp.float32
    ).reshape(tile_rows, tile_rows, channels)
    update = (gate * lin).astype(jnp.bfloat16)
    cot = cotangent.astype(jnp.float32)
    d_lin = (cot * gate).astype(jnp.bfloat16)
    d_gpre = (cot * lin * gate * (1.0 - gate)).astype(jnp.bfloat16)
    d_tnorm = jnp.dot(
        d_lin.reshape(cells, channels), out_weight.T, preferred_element_type=jnp.float32
    ).reshape(tile_rows, tile_rows, hidden)
    d_tri = norm_back(d_tnorm * out_gain, unit_tri, inv_tri).astype(jnp.bfloat16)
    grad_rows = lax.all_gather(d_tri, "col", axis=1, tiled=True)
    back_panel = lax.all_gather(right, "row", axis=0, tiled=True)
    piece = grad_rows
    d_right = lax.psum_scatter(
        jnp.einsum("ijh,ikh->jkh", piece, left, preferred_element_type=jnp.float32),
        "row",
        scatter_dimension=0,
        tiled=True,
    )
    d_left = jnp.einsum("ijh,jkh->ikh", grad_rows, back_panel, preferred_element_type=jnp.float32)
    d_proj = jnp.concatenate(
        [
            d_left * pair_keep * left_val * left_sig * (1.0 - left_sig),
            d_left * pair_keep * left_sig,
            d_right * pair_keep * right_val * right_sig * (1.0 - right_sig),
            d_right * pair_keep * right_sig,
        ],
        axis=-1,
    ).astype(jnp.bfloat16)
    d_normed = jnp.dot(
        d_proj.reshape(cells, 4 * hidden), proj_weight.T, preferred_element_type=jnp.float32
    )
    d_normed = d_normed + jnp.dot(
        d_gpre.reshape(cells, channels), gate_weight.T, preferred_element_type=jnp.float32
    )
    pair_grad = norm_back(
        d_normed.reshape(tile_rows, tile_rows, channels) * in_gain, unit_in, inv_in
    )
    return (update, pair_grad)


F32 = jnp.float32
BF16 = jnp.bfloat16
LANES = 128
ORDER = (6, 4, 11, 7, 5, 0, 15, 12, 14, 8, 1, 10, 9, 13, 2, 3)
PLACE = tuple(ORDER.index(device) for device in range(len(ORDER)))


def dot(a, b, dims):
    return lax.dot_general(a, b, ((dims[:1], dims[1:]), ((), ())), preferred_element_type=F32)


def column(gain):
    n = gain.shape[1]
    return jnp.broadcast_to(gain, (n, n)).T


def spread(col, width):
    return jnp.concatenate([col] * (width // col.shape[1]), axis=1)


def unit_rows(values):
    n = values.shape[0]
    centred = values - jnp.sum(values, axis=0, keepdims=True) * (1.0 / n)
    inv = lax.rsqrt(jnp.sum(centred * centred, axis=0, keepdims=True) * (1.0 / n) + eps_norm)
    return centred * inv, inv


def unit_back(q, unit, inv):
    n = q.shape[0]
    first = jnp.sum(q, axis=0, keepdims=True) * (1.0 / n)
    second = jnp.sum(q * unit, axis=0, keepdims=True) * (1.0 / n)
    return inv * (q - first - unit * second)


def one_hot(at):
    return jnp.where(at, 1.0, 0.0).astype(BF16)


def block_swap():
    width = LANES // 4
    row = lax.broadcasted_iota(jnp.int32, (width, LANES), 0)
    lane = lax.broadcasted_iota(jnp.int32, (width, LANES), 1)
    none = jnp.zeros((width, LANES), BF16)
    to = [one_hot(row + width * c == lane) for c in range(4)]
    return jnp.concatenate(
        [jnp.concatenate([to[c] if n == p else none for n in range(4)], axis=1) for c in range(4) for p in range(4)],
        axis=0,
    )


def keep_row(valid, tile, cells):
    n = valid.ref.shape[1]
    groups, rows = cells // n, n // tile
    token = lax.broadcasted_iota(jnp.int32, (n, n), 0)
    lane = lax.broadcasted_iota(jnp.int32, (n, n), 1)
    place = lax.broadcasted_iota(jnp.int32, (groups, n), 1) - lax.axis_index("row") * tile
    group = rows * lax.broadcasted_iota(jnp.int32, (groups, n), 0)
    inside = jnp.logical_and(place >= group, place < group + rows)
    first = one_hot(lax.rem(token, rows) == lax.div(lane, tile))
    second = one_hot(token - lax.axis_index("col") * tile == lax.rem(lane, tile))
    v = jnp.broadcast_to(valid.ready()[...].astype(F32), (groups, n))
    own = jnp.where(inside, v, 0.0).astype(BF16)
    keep = dot(own, first, (1, 0)) * dot(v.astype(BF16), second, (1, 0))
    return jnp.concatenate([keep[g : g + 1] for g in range(groups)], axis=1)


def normed_of(pair, in_gain):
    unit, inv = unit_rows(pair.ready()[...].astype(F32).T)
    normed = (unit * spread(column(in_gain.ready()[...]), unit.shape[1])).astype(BF16)
    return normed, unit, inv


def project_kernel(tile, parts, valid, in_gain, proj_weight, pair, out):
    cells, channels = pair.ref.shape
    hidden = proj_weight.ref.shape[1] // 4
    shards, both, _ = out.ref.shape
    per = both // 2
    keep = keep_row(valid, tile, cells)
    normed, _, _ = normed_of(pair, in_gain)
    weights = proj_weight.ready()[...].T
    share = hidden // parts
    for part in range(parts):
        rows = [weights[block * hidden + part * share : block * hidden + (part + 1) * share] for block in range(4)]
        proj = dot(jnp.concatenate(rows, axis=0), normed, (1, 0))
        left = jax.nn.sigmoid(proj[:share]) * proj[share : 2 * share] * keep
        right = jax.nn.sigmoid(proj[2 * share : 3 * share]) * proj[3 * share :] * keep
        for s in range(shards // parts):
            own = slice(s * per, (s + 1) * per)
            out.ref[part * shards // parts + s] = jnp.concatenate([left[own], right[own]], axis=0).astype(BF16)
        out.send(part)


def gate_of(normed, cot, gate_weight):
    gate = jax.nn.sigmoid(dot(gate_weight.ready()[...].T, normed, (1, 0)))
    return gate, cot.ready()[...].astype(F32).T


def gate_kernel(pair, cot, in_gain, gate_weight, out_gain, out_weight, q_ref):
    normed, _, _ = normed_of(pair, in_gain)
    gate, cot_rows = gate_of(normed, cot, gate_weight)
    q = dot(out_weight.ready()[...], (cot_rows * gate).astype(BF16), (1, 0))
    q_ref[...] = q * spread(column(out_gain.ready()[...]), q.shape[1])


def tri_kernel(grid_rows, recv_ref, out_ref, left, right, rows, tri):
    devices, both, cells = recv_ref.shape
    per = both // 2
    n = left.ref.shape[1]
    tile = n // grid_rows
    groups = cells // LANES
    swap = block_swap()
    for r in range(grid_rows):
        x = jnp.concatenate(
            [
                jnp.concatenate(
                    [recv_ref[PLACE[grid_rows * r + c], :, g * LANES : (g + 1) * LANES] for c in range(grid_rows)], axis=1
                )
                for g in range(groups)
            ],
            axis=0,
        )
        y = dot(x, swap, (1, 0))
        for g in range(groups):
            for p in range(grid_rows):
                at = (r * tile + g * grid_rows + p) * both
                rows[at : at + both, :] = y[g * both : (g + 1) * both, p * LANES : (p + 1) * LANES]
    for h in range(per):
        left.ref[h] = rows[pl.ds(h, n, stride=both), :].astype(BF16)
        right.ref[h] = rows[pl.ds(per + h, n, stride=both), :].astype(BF16)
    left.send()
    right.send()
    for h in range(per):
        tri[pl.ds(h, n, stride=per), :] = dot(left.ref[h], right.ref[h], (1, 1))
    half = groups // 2
    for r in range(grid_rows):
        x = jnp.concatenate(
            [
                jnp.concatenate(
                    [
                        tri[at : at + per, :]
                        for p in range(grid_rows)
                        for at in [(r * tile + (g + k * half) * grid_rows + p) * per]
                    ],
                    axis=1,
                )
                for g in range(half)
                for k in range(2)
            ],
            axis=0,
        )
        y = dot(x.astype(BF16), swap, (1, 0)).astype(BF16)
        for g in range(half):
            for c in range(grid_rows):
                out_ref[PLACE[grid_rows * r + c], :, g * LANES : (g + 1) * LANES] = y[
                    g * both : (g + 1) * both, c * LANES : (c + 1) * LANES
                ]


def halves_of(recv_ref):
    shards, both, width = recv_ref.shape
    x = recv_ref[...].astype(F32)
    rows = shards * both // 2
    return jnp.concatenate(
        [x[:, : both // 2].reshape(rows, width), x[:, both // 2 :].reshape(rows, width)], axis=1
    )


def d_tri_kernel(recv_ref, q_ref, out_ref):
    shards, both, width = recv_ref.shape
    unit, inv = unit_rows(halves_of(recv_ref))
    d_tri = unit_back(q_ref[...], unit, inv)
    out_ref[...] = jnp.concatenate(
        [d_tri[:, :width].reshape(shards, both // 2, width), d_tri[:, width:].reshape(shards, both // 2, width)],
        axis=1,
    ).astype(BF16)


def update_kernel(
    tile, tri, out_gain, out_weight, pair, cot, valid, in_gain, gate_weight, proj_weight,
    unit_ref, inv_ref, factor_ref, update,
):
    normed, unit, inv = normed_of(pair, in_gain)
    unit_ref[...] = unit
    inv_ref[...] = inv
    gate, cot_rows = gate_of(normed, cot, gate_weight)
    unit_tri, _ = unit_rows(halves_of(tri.ready()))
    tnorm = (unit_tri * spread(column(out_gain.ready()[...]), unit.shape[1])).astype(BF16)
    lin = dot(out_weight.ready()[...].T, tnorm, (1, 0))
    update.ref[...] = (gate * lin).T.astype(BF16)
    update.send()
    factor_ref[4] = (cot_rows * lin * gate * (1.0 - gate)).astype(BF16)
    hidden = proj_weight.ref.shape[1] // 4
    keep = keep_row(valid, tile, unit.shape[1])
    weights = proj_weight.ready()
    for side in range(2):
        weight = weights[:, 2 * hidden * side : 2 * hidden * (side + 1)].T
        proj = dot(weight, normed, (1, 0))
        sig = jax.nn.sigmoid(proj[:hidden])
        factor_ref[2 * side] = (keep * proj[hidden:] * sig * (1.0 - sig)).astype(BF16)
        factor_ref[2 * side + 1] = (keep * sig).astype(BF16)


def sides_kernel(grid_rows, recv_ref, left, right, out, d_tri, rows):
    devices, both, cells = out.ref.shape
    per = both // 2
    n = left.ref.shape[1]
    tile = n // grid_rows
    groups = cells // LANES
    half = groups // 2
    swap = block_swap()
    for r in range(grid_rows):
        x = jnp.concatenate(
            [
                jnp.concatenate(
                    [recv_ref[PLACE[grid_rows * r + c], :, g * LANES : (g + 1) * LANES] for c in range(grid_rows)], axis=1
                )
                for g in range(half)
            ],
            axis=0,
        )
        y = dot(x, swap, (1, 0))
        for g in range(half):
            for k in range(2):
                for p in range(grid_rows):
                    at = (r * tile + (g + k * half) * grid_rows + p) * per
                    d_tri[at : at + per, :] = y[
                        g * both + k * per : g * both + (k + 1) * per, p * LANES : (p + 1) * LANES
                    ]
    left_ref, right_ref = left.ready(), right.ready()
    for h in range(per):
        grad = d_tri[pl.ds(h, n, stride=per), :].astype(BF16)
        rows[pl.ds(h, n, stride=both), :] = dot(grad, right_ref[h], (1, 0))
        rows[pl.ds(per + h, n, stride=both), :] = dot(grad, left_ref[h], (0, 0))
    for r in range(grid_rows):
        x = jnp.concatenate(
            [
                jnp.concatenate(
                    [
                        rows[at : at + both, :]
                        for p in range(grid_rows)
                        for at in [(r * tile + g * grid_rows + p) * both]
                    ],
                    axis=1,
                )
                for g in range(groups)
            ],
            axis=0,
        )
        y = dot(x.astype(BF16), swap, (1, 0)).astype(BF16)
        for c in range(grid_rows):
            place = PLACE[grid_rows * r + c]
            for g in range(groups):
                out.ref[place, :, g * LANES : (g + 1) * LANES] = y[
                    g * both : (g + 1) * both, c * LANES : (c + 1) * LANES
                ]
            out.send(place)


def pair_grad_kernel(parts, recv_ref, factor_ref, unit_ref, inv_ref, in_gain, proj_weight, gate_weight, out):
    shards, both, cells = recv_ref.shape
    hidden = shards * both // 2
    width = cells // parts
    gain = spread(column(in_gain.ready()[...]), width)
    weights, gate_weights = proj_weight.ready()[...], gate_weight.ready()[...]
    for part in range(parts):
        lanes = slice(part * width, (part + 1) * width)
        x = recv_ref[:, :, lanes].astype(F32)
        grads = (x[:, : both // 2].reshape(hidden, width), x[:, both // 2 :].reshape(hidden, width))
        d_proj = jnp.concatenate(
            [
                (grad * factor_ref[2 * side + k, :, lanes].astype(F32)).astype(BF16)
                for side, grad in enumerate(grads)
                for k in range(2)
            ],
            axis=0,
        )
        d_normed = dot(weights, d_proj, (1, 0)) + dot(gate_weights, factor_ref[4, :, lanes], (1, 0))
        out.ref[lanes, :] = unit_back(d_normed * gain, unit_ref[:, lanes], inv_ref[:, lanes]).T
        out.send(part)


class Arriving:
    def __init__(self, source, ref, sems, parts):
        size = ref.shape[0] // parts
        cuts = [pl.ds(part * size, size) for part in range(parts)]
        self.ref = ref
        self.copies = [pltpu.make_async_copy(source.at[cut], ref.at[cut], sem) for cut, sem in zip(cuts, sems)]
        for copy in self.copies:
            copy.start()
        self.waiting = set(range(parts))

    def ready(self, part=None):
        for one in sorted(self.waiting) if part is None else [part]:
            if one in self.waiting:
                self.copies[one].wait()
                self.waiting.remove(one)
        return self.ref


class Leaving:
    def __init__(self, target, ref, sems, parts, dim):
        size = ref.shape[dim] // parts
        cuts = [(slice(None),) * dim + (pl.ds(part * size, size),) for part in range(parts)]
        self.ref = ref
        self.copies = [pltpu.make_async_copy(ref.at[cut], target.at[cut], sem) for cut, sem in zip(cuts, sems)]

    def send(self, part=0):
        self.copies[part].start()


def call(kernel, outs, args, flops, scratch=(), far=(), far_outs=(), room=24):
    outs, args, scratch = list(outs), list(args), list(scratch)
    far = [one if isinstance(one, tuple) else (one, 1) for one in far]
    far_outs = [one if isinstance(one, tuple) else (one, 1, 0) for one in far_outs]
    far_arrays, far_shapes = [one[0] for one in far], [one[0] for one in far_outs]
    counts = [len(args), len(far), len(outs), len(far_outs), len(far), len(far_outs), len(scratch)]

    def body(*refs):
        groups, at = [], 0
        for count in counts:
            groups.append(list(refs[at : at + count]))
            at += count
        near_in, far_in, near_out, far_out, held, leaving, rest = groups
        sems = refs[at]
        used = 0
        arrivals, departures = [], []
        for source, ref, (_, parts) in zip(far_in, held, far):
            arrivals.append(Arriving(source, ref, [sems.at[used + k] for k in range(parts)], parts))
            used += parts
        for target, ref, (_, parts, dim) in zip(far_out, leaving, far_outs):
            departures.append(Leaving(target, ref, [sems.at[used + k] for k in range(parts)], parts, dim))
            used += parts
        kernel(*near_in, *arrivals, *near_out, *departures, *rest)
        for one in arrivals:
            one.ready()
        for one in departures:
            for copy in one.copies:
                copy.wait()

    near_spec, far_spec = pl.BlockSpec(memory_space=pltpu.VMEM), pl.BlockSpec(memory_space=pltpu.HBM)
    moved = sum(a.size * a.dtype.itemsize for a in args + far_arrays + outs + far_shapes)
    return pl.pallas_call(
        body,
        out_shape=tuple(outs + far_shapes),
        in_specs=[near_spec] * len(args) + [far_spec] * len(far),
        out_specs=tuple([near_spec] * len(outs) + [far_spec] * len(far_outs)),
        scratch_shapes=[pltpu.VMEM(a.shape, a.dtype) for a in far_arrays + far_shapes]
        + scratch
        + [pltpu.SemaphoreType.DMA((max(1, sum(one[1] for one in far + far_outs)),))],
        compiler_params=pltpu.CompilerParams(vmem_limit_bytes=int(room * 2**20)),
        cost_estimate=pl.CostEstimate(flops=flops, bytes_accessed=moved, transcendentals=0),
    )(*args, *far_arrays)


def by_channel(pair, cotangent, valid, in_gain, proj_weight, gate_weight, out_gain, out_weight):
    tile, _, channels = pair.shape
    hidden = out_weight.shape[0]
    cells = tile * tile
    grid_rows = lax.axis_size("row")
    devices = grid_rows * lax.axis_size("col")
    per = hidden // devices
    n = tile * grid_rows
    shape = lambda dims, dtype: jax.ShapeDtypeStruct(dims, dtype)
    whole = lambda x: lax.all_to_all(x, ("row", "col"), 0, 0, axis_index_groups=[ORDER], tiled=True)
    flat = pair.reshape(cells, channels)
    flat_cot = cotangent.reshape(cells, channels)
    valid_row = valid.reshape(1, -1)
    in_row = in_gain.reshape(1, -1)
    out_row = out_gain.reshape(1, -1)
    both = 2 * per
    plane = shape((channels, cells), F32)

    (sides,) = call(
        functools.partial(project_kernel, tile, 4),
        [],
        (),
        2 * cells * channels * 4 * hidden,
        far=(valid_row, in_row, proj_weight, flat),
        far_outs=[(shape((devices, both, cells), BF16), 4, 0)],
        room=62,
    )
    sides, flat_2, flat_cot_2 = lax.optimization_barrier((sides, flat, flat_cot))
    sides = whole(sides)
    (q,) = call(
        gate_kernel,
        [plane],
        (),
        2 * cells * channels * 2 * hidden,
        far=(flat_2, flat_cot_2, in_row, gate_weight, out_row, out_weight),
    )
    sides, q = lax.optimization_barrier((sides, q))
    tri, left, right = call(
        functools.partial(tri_kernel, grid_rows),
        [shape((devices, both, cells // 2), BF16)],
        (sides,),
        2 * per * n * n * n,
        [pltpu.VMEM((n * both, n), F32), pltpu.VMEM((n * per, n), F32)],
        far_outs=[shape((per, n, n), BF16)] * 2,
    )
    tri = whole(tri)
    (d_tri,) = call(
        d_tri_kernel,
        [shape((devices, both, cells // 2), BF16)],
        (tri, q),
        20 * cells * hidden,
    )
    d_tri = whole(d_tri)
    (d_sides,) = call(
        functools.partial(sides_kernel, grid_rows),
        [],
        (d_tri,),
        4 * per * n * n * n,
        [pltpu.VMEM((n * per, n), F32), pltpu.VMEM((n * both, n), F32)],
        far=(left, right),
        far_outs=[(shape((devices, both, cells), BF16), devices, 0)],
    )
    d_sides, flat_4, flat_cot_4, tri = lax.optimization_barrier((d_sides, flat, flat_cot, tri))
    d_sides = whole(d_sides)
    unit, inv, factors, update = call(
        functools.partial(update_kernel, tile),
        [plane, shape((1, cells), F32), shape((5, hidden, cells), BF16)],
        (),
        2 * cells * channels * 6 * hidden,
        far=(tri, out_row, out_weight, flat_4, flat_cot_4, valid_row, in_row, gate_weight, proj_weight),
        far_outs=[shape((cells, channels), BF16)],
    )
    (pair_grad,) = call(
        functools.partial(pair_grad_kernel, 4),
        [],
        (d_sides, factors, unit, inv),
        2 * cells * channels * 5 * hidden,
        far=(in_row, proj_weight, gate_weight),
        far_outs=[(shape((cells, channels), F32), 4, 0)],
    )
    return (update.reshape(pair.shape), pair_grad.reshape(pair.shape))


def fits(pair, out_weight):
    rows, cols = lax.axis_size("row"), lax.axis_size("col")
    tile, tile_cols, channels = pair.shape
    hidden = out_weight.shape[0]
    return (
        rows == cols == 4
        and tile == tile_cols
        and tile * rows == LANES
        and channels == LANES
        and hidden == 8 * rows * cols
    )


def step(pair, cotangent, valid, in_gain, proj_weight, gate_weight, out_gain, out_weight):
    plan = by_channel if fits(pair, out_weight) else on_device
    return plan(pair, cotangent, valid, in_gain, proj_weight, gate_weight, out_gain, out_weight)


def solution(mesh):
    placed = (
        P(("replica", "row"), "col", None),
        P(("replica", "row"), "col", None),
        P("replica"),
        P(),
        P(),
        P(),
        P(),
        P(),
    )
    return jax.shard_map(
        step,
        mesh=mesh,
        in_specs=placed,
        out_specs=(P(("replica", "row"), "col", None), P(("replica", "row"), "col", None)),
        check_vma=False,
    )
```

```python
import functools

import jax
import jax.numpy as jnp
from jax import lax
from jax.experimental import pallas as pl
from jax.experimental.pallas import tpu as pltpu
from jax.sharding import PartitionSpec as P

eps_norm = 1e-05


def layer_norm(values, gain):
    mean_val = jnp.mean(values, axis=-1, keepdims=True)
    centred = values - mean_val
    inv_std = lax.rsqrt(jnp.mean(centred * centred, axis=-1, keepdims=True) + eps_norm)
    unit = centred * inv_std
    return (unit * gain, unit, inv_std)


def norm_back(grad_unit, unit, inv_std):
    first = jnp.mean(grad_unit, axis=-1, keepdims=True)
    second = jnp.mean(grad_unit * unit, axis=-1, keepdims=True)
    return inv_std * (grad_unit - first - unit * second)


def on_device(pair, cotangent, valid, in_gain, proj_weight, gate_weight, out_gain, out_weight):
    tile_rows = pair.shape[0]
    channels = pair.shape[2]
    hidden = out_weight.shape[0]
    cells = tile_rows * tile_rows
    keeper = valid.astype(jnp.float32)
    row_keep = lax.dynamic_slice_in_dim(keeper, lax.axis_index("row") * tile_rows, tile_rows)
    col_keep = lax.dynamic_slice_in_dim(keeper, lax.axis_index("col") * tile_rows, tile_rows)
    pair_keep = (row_keep[:, None] * col_keep[None, :])[:, :, None]
    normed_f, unit_in, inv_in = layer_norm(pair.astype(jnp.float32), in_gain)
    normed = normed_f.astype(jnp.bfloat16)
    flat = normed.reshape(cells, channels)
    proj = jnp.dot(flat, proj_weight, preferred_element_type=jnp.float32).reshape(
        tile_rows, tile_rows, 4 * hidden
    )
    left_sig = jax.nn.sigmoid(proj[..., :hidden])
    left_val = proj[..., hidden : 2 * hidden]
    right_sig = jax.nn.sigmoid(proj[..., 2 * hidden : 3 * hidden])
    right_val = proj[..., 3 * hidden :]
    left = (left_sig * left_val * pair_keep).astype(jnp.bfloat16)
    right = (right_sig * right_val * pair_keep).astype(jnp.bfloat16)
    panel = lax.all_gather(right, "row", axis=0, tiled=True)
    piece = panel
    tri = jnp.swapaxes(
        lax.psum_scatter(
            jnp.einsum("ikh,jkh->jih", left, piece, preferred_element_type=jnp.float32),
            "col",
            scatter_dimension=0,
            tiled=True,
        ),
        0,
        1,
    )
    tnorm_f, unit_tri, inv_tri = layer_norm(tri, out_gain)
    tnorm = tnorm_f.astype(jnp.bfloat16)
    gate = jax.nn.sigmoid(jnp.dot(flat, gate_weight, preferred_element_type=jnp.float32)).reshape(
        tile_rows, tile_rows, channels
    )
    lin = jnp.dot(
        tnorm.reshape(cells, hidden), out_weight, preferred_element_type=jnp.float32
    ).reshape(tile_rows, tile_rows, channels)
    update = (gate * lin).astype(jnp.bfloat16)
    cot = cotangent.astype(jnp.float32)
    d_lin = (cot * gate).astype(jnp.bfloat16)
    d_gpre = (cot * lin * gate * (1.0 - gate)).astype(jnp.bfloat16)
    d_tnorm = jnp.dot(
        d_lin.reshape(cells, channels), out_weight.T, preferred_element_type=jnp.float32
    ).reshape(tile_rows, tile_rows, hidden)
    d_tri = norm_back(d_tnorm * out_gain, unit_tri, inv_tri).astype(jnp.bfloat16)
    grad_rows = lax.all_gather(d_tri, "col", axis=1, tiled=True)
    back_panel = lax.all_gather(right, "row", axis=0, tiled=True)
    piece = grad_rows
    d_right = lax.psum_scatter(
        jnp.einsum("ijh,ikh->jkh", piece, left, preferred_element_type=jnp.float32),
        "row",
        scatter_dimension=0,
        tiled=True,
    )
    d_left = jnp.einsum("ijh,jkh->ikh", grad_rows, back_panel, preferred_element_type=jnp.float32)
    d_proj = jnp.concatenate(
        [
            d_left * pair_keep * left_val * left_sig * (1.0 - left_sig),
            d_left * pair_keep * left_sig,
            d_right * pair_keep * right_val * right_sig * (1.0 - right_sig),
            d_right * pair_keep * right_sig,
        ],
        axis=-1,
    ).astype(jnp.bfloat16)
    d_normed = jnp.dot(
        d_proj.reshape(cells, 4 * hidden), proj_weight.T, preferred_element_type=jnp.float32
    )
    d_normed = d_normed + jnp.dot(
        d_gpre.reshape(cells, channels), gate_weight.T, preferred_element_type=jnp.float32
    )
    pair_grad = norm_back(
        d_normed.reshape(tile_rows, tile_rows, channels) * in_gain, unit_in, inv_in
    )
    return (update, pair_grad)


F32 = jnp.float32
BF16 = jnp.bfloat16
LANES = 128
ORDER = (6, 7, 11, 0, 12, 2, 3, 5, 14, 8, 1, 10, 9, 13, 4, 15)
PLACE = tuple(ORDER.index(device) for device in range(len(ORDER)))


def dot(a, b, dims):
    return lax.dot_general(a, b, ((dims[:1], dims[1:]), ((), ())), preferred_element_type=F32)


def column(gain):
    n = gain.shape[1]
    return jnp.broadcast_to(gain, (n, n)).T


def spread(col, width):
    return jnp.concatenate([col] * (width // col.shape[1]), axis=1)


def unit_rows(values):
    n = values.shape[0]
    centred = values - jnp.sum(values, axis=0, keepdims=True) * (1.0 / n)
    inv = lax.rsqrt(jnp.sum(centred * centred, axis=0, keepdims=True) * (1.0 / n) + eps_norm)
    return centred * inv, inv


def unit_back(q, unit, inv):
    n = q.shape[0]
    first = jnp.sum(q, axis=0, keepdims=True) * (1.0 / n)
    second = jnp.sum(q * unit, axis=0, keepdims=True) * (1.0 / n)
    return inv * (q - first - unit * second)


def one_hot(at):
    return jnp.where(at, 1.0, 0.0).astype(BF16)


def block_swap():
    width = LANES // 4
    row = lax.broadcasted_iota(jnp.int32, (width, LANES), 0)
    lane = lax.broadcasted_iota(jnp.int32, (width, LANES), 1)
    none = jnp.zeros((width, LANES), BF16)
    to = [one_hot(row + width * c == lane) for c in range(4)]
    return jnp.concatenate(
        [jnp.concatenate([to[c] if n == p else none for n in range(4)], axis=1) for c in range(4) for p in range(4)],
        axis=0,
    )


def keep_row(valid, tile, cells):
    n = valid.ref.shape[1]
    groups, rows = cells // n, n // tile
    token = lax.broadcasted_iota(jnp.int32, (n, n), 0)
    lane = lax.broadcasted_iota(jnp.int32, (n, n), 1)
    place = lax.broadcasted_iota(jnp.int32, (groups, n), 1) - lax.axis_index("row") * tile
    group = rows * lax.broadcasted_iota(jnp.int32, (groups, n), 0)
    inside = jnp.logical_and(place >= group, place < group + rows)
    first = one_hot(lax.rem(token, rows) == lax.div(lane, tile))
    second = one_hot(token - lax.axis_index("col") * tile == lax.rem(lane, tile))
    v = jnp.broadcast_to(valid.ready()[...].astype(F32), (groups, n))
    own = jnp.where(inside, v, 0.0).astype(BF16)
    keep = dot(own, first, (1, 0)) * dot(v.astype(BF16), second, (1, 0))
    return jnp.concatenate([keep[g : g + 1] for g in range(groups)], axis=1)


def normed_of(pair, in_gain):
    unit, inv = unit_rows(pair.ready()[...].astype(F32).T)
    normed = (unit * spread(column(in_gain.ready()[...]), unit.shape[1])).astype(BF16)
    return normed, unit, inv


def project_kernel(tile, parts, valid, in_gain, proj_weight, pair, out):
    cells, channels = pair.ref.shape
    hidden = proj_weight.ref.shape[1] // 4
    shards, both, _ = out.ref.shape
    per = both // 2
    keep = keep_row(valid, tile, cells)
    normed, _, _ = normed_of(pair, in_gain)
    weights = proj_weight.ready()[...].T
    share = hidden // parts
    for part in range(parts):
        rows = [weights[block * hidden + part * share : block * hidden + (part + 1) * share] for block in range(4)]
        proj = dot(jnp.concatenate(rows, axis=0), normed, (1, 0))
        left = jax.nn.sigmoid(proj[:share]) * proj[share : 2 * share] * keep
        right = jax.nn.sigmoid(proj[2 * share : 3 * share]) * proj[3 * share :] * keep
        for s in range(shards // parts):
            own = slice(s * per, (s + 1) * per)
            out.ref[part * shards // parts + s] = jnp.concatenate([left[own], right[own]], axis=0).astype(BF16)
        out.send(part)


def gate_of(normed, cot, gate_weight):
    gate = jax.nn.sigmoid(dot(gate_weight.ready()[...].T, normed, (1, 0)))
    return gate, cot.ready()[...].astype(F32).T


def gate_kernel(pair, cot, in_gain, gate_weight, out_gain, out_weight, q_ref):
    normed, _, _ = normed_of(pair, in_gain)
    gate, cot_rows = gate_of(normed, cot, gate_weight)
    q = dot(out_weight.ready()[...], (cot_rows * gate).astype(BF16), (1, 0))
    q_ref[...] = q * spread(column(out_gain.ready()[...]), q.shape[1])


def tri_kernel(grid_rows, recv_ref, out_ref, left_ref, right_ref, rows, tri):
    devices, both, cells = recv_ref.shape
    per = both // 2
    n = left_ref.shape[1]
    tile = n // grid_rows
    groups = cells // LANES
    swap = block_swap()
    for r in range(grid_rows):
        x = jnp.concatenate(
            [
                jnp.concatenate(
                    [recv_ref[PLACE[grid_rows * r + c], :, g * LANES : (g + 1) * LANES] for c in range(grid_rows)], axis=1
                )
                for g in range(groups)
            ],
            axis=0,
        )
        y = dot(x, swap, (1, 0))
        for g in range(groups):
            for p in range(grid_rows):
                at = (r * tile + g * grid_rows + p) * both
                rows[at : at + both, :] = y[g * both : (g + 1) * both, p * LANES : (p + 1) * LANES]
    for h in range(per):
        left = rows[pl.ds(h, n, stride=both), :].astype(BF16)
        right = rows[pl.ds(per + h, n, stride=both), :].astype(BF16)
        left_ref[h] = left
        right_ref[h] = right
        tri[pl.ds(h, n, stride=per), :] = dot(left, right, (1, 1))
    half = groups // 2
    for r in range(grid_rows):
        x = jnp.concatenate(
            [
                jnp.concatenate(
                    [
                        tri[at : at + per, :]
                        for p in range(grid_rows)
                        for at in [(r * tile + (g + k * half) * grid_rows + p) * per]
                    ],
                    axis=1,
                )
                for g in range(half)
                for k in range(2)
            ],
            axis=0,
        )
        y = dot(x.astype(BF16), swap, (1, 0)).astype(BF16)
        for g in range(half):
            for c in range(grid_rows):
                out_ref[PLACE[grid_rows * r + c], :, g * LANES : (g + 1) * LANES] = y[
                    g * both : (g + 1) * both, c * LANES : (c + 1) * LANES
                ]


def halves_of(recv_ref):
    shards, both, width = recv_ref.shape
    x = recv_ref[...].astype(F32)
    rows = shards * both // 2
    return jnp.concatenate(
        [x[:, : both // 2].reshape(rows, width), x[:, both // 2 :].reshape(rows, width)], axis=1
    )


def d_tri_kernel(recv_ref, q_ref, out_ref):
    shards, both, width = recv_ref.shape
    unit, inv = unit_rows(halves_of(recv_ref))
    d_tri = unit_back(q_ref[...], unit, inv)
    out_ref[...] = jnp.concatenate(
        [d_tri[:, :width].reshape(shards, both // 2, width), d_tri[:, width:].reshape(shards, both // 2, width)],
        axis=1,
    ).astype(BF16)


def update_kernel(
    tile, tri, out_gain, out_weight, pair, cot, valid, in_gain, gate_weight, proj_weight,
    unit_ref, inv_ref, factor_ref, update,
):
    normed, unit, inv = normed_of(pair, in_gain)
    unit_ref[...] = unit
    inv_ref[...] = inv
    gate, cot_rows = gate_of(normed, cot, gate_weight)
    unit_tri, _ = unit_rows(halves_of(tri.ready()))
    tnorm = (unit_tri * spread(column(out_gain.ready()[...]), unit.shape[1])).astype(BF16)
    lin = dot(out_weight.ready()[...].T, tnorm, (1, 0))
    update.ref[...] = (gate * lin).T.astype(BF16)
    update.send()
    factor_ref[4] = (cot_rows * lin * gate * (1.0 - gate)).astype(BF16)
    hidden = proj_weight.ref.shape[1] // 4
    keep = keep_row(valid, tile, unit.shape[1])
    weights = proj_weight.ready()
    for side in range(2):
        weight = weights[:, 2 * hidden * side : 2 * hidden * (side + 1)].T
        proj = dot(weight, normed, (1, 0))
        sig = jax.nn.sigmoid(proj[:hidden])
        factor_ref[2 * side] = (keep * proj[hidden:] * sig * (1.0 - sig)).astype(BF16)
        factor_ref[2 * side + 1] = (keep * sig).astype(BF16)


def sides_kernel(grid_rows, recv_ref, left_ref, right_ref, out, d_tri, rows):
    devices, both, cells = out.ref.shape
    per = both // 2
    n = left_ref.shape[1]
    tile = n // grid_rows
    groups = cells // LANES
    half = groups // 2
    swap = block_swap()
    for r in range(grid_rows):
        x = jnp.concatenate(
            [
                jnp.concatenate(
                    [recv_ref[PLACE[grid_rows * r + c], :, g * LANES : (g + 1) * LANES] for c in range(grid_rows)], axis=1
                )
                for g in range(half)
            ],
            axis=0,
        )
        y = dot(x, swap, (1, 0))
        for g in range(half):
            for k in range(2):
                for p in range(grid_rows):
                    at = (r * tile + (g + k * half) * grid_rows + p) * per
                    d_tri[at : at + per, :] = y[
                        g * both + k * per : g * both + (k + 1) * per, p * LANES : (p + 1) * LANES
                    ]
    for h in range(per):
        grad = d_tri[pl.ds(h, n, stride=per), :].astype(BF16)
        rows[pl.ds(h, n, stride=both), :] = dot(grad, right_ref[h], (1, 0))
        rows[pl.ds(per + h, n, stride=both), :] = dot(grad, left_ref[h], (0, 0))
    for r in range(grid_rows):
        x = jnp.concatenate(
            [
                jnp.concatenate(
                    [
                        rows[at : at + both, :]
                        for p in range(grid_rows)
                        for at in [(r * tile + g * grid_rows + p) * both]
                    ],
                    axis=1,
                )
                for g in range(groups)
            ],
            axis=0,
        )
        y = dot(x.astype(BF16), swap, (1, 0)).astype(BF16)
        for c in range(grid_rows):
            place = PLACE[grid_rows * r + c]
            for g in range(groups):
                out.ref[place, :, g * LANES : (g + 1) * LANES] = y[
                    g * both : (g + 1) * both, c * LANES : (c + 1) * LANES
                ]
            out.send(place)


def pair_grad_kernel(parts, recv_ref, factor_ref, unit_ref, inv_ref, in_gain, proj_weight, gate_weight, out):
    shards, both, cells = recv_ref.shape
    hidden = shards * both // 2
    width = cells // parts
    gain = spread(column(in_gain.ready()[...]), width)
    weights, gate_weights = proj_weight.ready()[...], gate_weight.ready()[...]
    for part in range(parts):
        lanes = slice(part * width, (part + 1) * width)
        x = recv_ref[:, :, lanes].astype(F32)
        grads = (x[:, : both // 2].reshape(hidden, width), x[:, both // 2 :].reshape(hidden, width))
        d_proj = jnp.concatenate(
            [
                (grad * factor_ref[2 * side + k, :, lanes].astype(F32)).astype(BF16)
                for side, grad in enumerate(grads)
                for k in range(2)
            ],
            axis=0,
        )
        d_normed = dot(weights, d_proj, (1, 0)) + dot(gate_weights, factor_ref[4, :, lanes], (1, 0))
        out.ref[lanes, :] = unit_back(d_normed * gain, unit_ref[:, lanes], inv_ref[:, lanes]).T
        out.send(part)


class Arriving:
    def __init__(self, source, ref, sems, parts):
        size = ref.shape[0] // parts
        cuts = [pl.ds(part * size, size) for part in range(parts)]
        self.ref = ref
        self.copies = [pltpu.make_async_copy(source.at[cut], ref.at[cut], sem) for cut, sem in zip(cuts, sems)]
        for copy in self.copies:
            copy.start()
        self.waiting = set(range(parts))

    def ready(self, part=None):
        for one in sorted(self.waiting) if part is None else [part]:
            if one in self.waiting:
                self.copies[one].wait()
                self.waiting.remove(one)
        return self.ref


class Leaving:
    def __init__(self, target, ref, sems, parts, dim):
        size = ref.shape[dim] // parts
        cuts = [(slice(None),) * dim + (pl.ds(part * size, size),) for part in range(parts)]
        self.ref = ref
        self.copies = [pltpu.make_async_copy(ref.at[cut], target.at[cut], sem) for cut, sem in zip(cuts, sems)]

    def send(self, part=0):
        self.copies[part].start()


def call(kernel, outs, args, flops, scratch=(), far=(), far_outs=(), room=24):
    outs, args, scratch = list(outs), list(args), list(scratch)
    far = [one if isinstance(one, tuple) else (one, 1) for one in far]
    far_outs = [one if isinstance(one, tuple) else (one, 1, 0) for one in far_outs]
    far_arrays, far_shapes = [one[0] for one in far], [one[0] for one in far_outs]
    counts = [len(args), len(far), len(outs), len(far_outs), len(far), len(far_outs), len(scratch)]

    def body(*refs):
        groups, at = [], 0
        for count in counts:
            groups.append(list(refs[at : at + count]))
            at += count
        near_in, far_in, near_out, far_out, held, leaving, rest = groups
        sems = refs[at]
        used = 0
        arrivals, departures = [], []
        for source, ref, (_, parts) in zip(far_in, held, far):
            arrivals.append(Arriving(source, ref, [sems.at[used + k] for k in range(parts)], parts))
            used += parts
        for target, ref, (_, parts, dim) in zip(far_out, leaving, far_outs):
            departures.append(Leaving(target, ref, [sems.at[used + k] for k in range(parts)], parts, dim))
            used += parts
        kernel(*near_in, *arrivals, *near_out, *departures, *rest)
        for one in arrivals:
            one.ready()
        for one in departures:
            for copy in one.copies:
                copy.wait()

    near_spec, far_spec = pl.BlockSpec(memory_space=pltpu.VMEM), pl.BlockSpec(memory_space=pltpu.HBM)
    moved = sum(a.size * a.dtype.itemsize for a in args + far_arrays + outs + far_shapes)
    return pl.pallas_call(
        body,
        out_shape=tuple(outs + far_shapes),
        in_specs=[near_spec] * len(args) + [far_spec] * len(far),
        out_specs=tuple([near_spec] * len(outs) + [far_spec] * len(far_outs)),
        scratch_shapes=[pltpu.VMEM(a.shape, a.dtype) for a in far_arrays + far_shapes]
        + scratch
        + [pltpu.SemaphoreType.DMA((max(1, sum(one[1] for one in far + far_outs)),))],
        compiler_params=pltpu.CompilerParams(vmem_limit_bytes=int(room * 2**20)),
        cost_estimate=pl.CostEstimate(flops=flops, bytes_accessed=moved, transcendentals=0),
    )(*args, *far_arrays)


def by_channel(pair, cotangent, valid, in_gain, proj_weight, gate_weight, out_gain, out_weight):
    tile, _, channels = pair.shape
    hidden = out_weight.shape[0]
    cells = tile * tile
    grid_rows = lax.axis_size("row")
    devices = grid_rows * lax.axis_size("col")
    per = hidden // devices
    n = tile * grid_rows
    shape = lambda dims, dtype: jax.ShapeDtypeStruct(dims, dtype)
    whole = lambda x: lax.all_to_all(x, ("row", "col"), 0, 0, axis_index_groups=[ORDER], tiled=True)
    flat = pair.reshape(cells, channels)
    flat_cot = cotangent.reshape(cells, channels)
    valid_row = valid.reshape(1, -1)
    in_row = in_gain.reshape(1, -1)
    out_row = out_gain.reshape(1, -1)
    both = 2 * per
    plane = shape((channels, cells), F32)

    (sides,) = call(
        functools.partial(project_kernel, tile, 4),
        [],
        (),
        2 * cells * channels * 4 * hidden,
        far=(valid_row, in_row, proj_weight, flat),
        far_outs=[(shape((devices, both, cells), BF16), 4, 0)],
        room=62,
    )
    sides, flat_2, flat_cot_2 = lax.optimization_barrier((sides, flat, flat_cot))
    sides = whole(sides)
    (q,) = call(
        gate_kernel,
        [plane],
        (),
        2 * cells * channels * 2 * hidden,
        far=(flat_2, flat_cot_2, in_row, gate_weight, out_row, out_weight),
    )
    sides, q = lax.optimization_barrier((sides, q))
    tri, left, right = call(
        functools.partial(tri_kernel, grid_rows),
        [shape((devices, both, cells // 2), BF16), shape((per, n, n), BF16), shape((per, n, n), BF16)],
        (sides,),
        2 * per * n * n * n,
        [pltpu.VMEM((n * both, n), F32), pltpu.VMEM((n * per, n), F32)],
    )
    tri = whole(tri)
    (d_tri,) = call(
        d_tri_kernel,
        [shape((devices, both, cells // 2), BF16)],
        (tri, q),
        20 * cells * hidden,
    )
    d_tri = whole(d_tri)
    (d_sides,) = call(
        functools.partial(sides_kernel, grid_rows),
        [],
        (d_tri, left, right),
        4 * per * n * n * n,
        [pltpu.VMEM((n * per, n), F32), pltpu.VMEM((n * both, n), F32)],
        far_outs=[(shape((devices, both, cells), BF16), devices, 0)],
    )
    d_sides, flat_4, flat_cot_4, tri = lax.optimization_barrier((d_sides, flat, flat_cot, tri))
    d_sides = whole(d_sides)
    unit, inv, factors, update = call(
        functools.partial(update_kernel, tile),
        [plane, shape((1, cells), F32), shape((5, hidden, cells), BF16)],
        (),
        2 * cells * channels * 6 * hidden,
        far=(tri, out_row, out_weight, flat_4, flat_cot_4, valid_row, in_row, gate_weight, proj_weight),
        far_outs=[shape((cells, channels), BF16)],
    )
    (pair_grad,) = call(
        functools.partial(pair_grad_kernel, 4),
        [],
        (d_sides, factors, unit, inv),
        2 * cells * channels * 5 * hidden,
        far=(in_row, proj_weight, gate_weight),
        far_outs=[(shape((cells, channels), F32), 4, 0)],
    )
    return (update.reshape(pair.shape), pair_grad.reshape(pair.shape))


def fits(pair, out_weight):
    rows, cols = lax.axis_size("row"), lax.axis_size("col")
    tile, tile_cols, channels = pair.shape
    hidden = out_weight.shape[0]
    return (
        rows == cols == 4
        and tile == tile_cols
        and tile * rows == LANES
        and channels == LANES
        and hidden == 8 * rows * cols
    )


def step(pair, cotangent, valid, in_gain, proj_weight, gate_weight, out_gain, out_weight):
    plan = by_channel if fits(pair, out_weight) else on_device
    return plan(pair, cotangent, valid, in_gain, proj_weight, gate_weight, out_gain, out_weight)


def solution(mesh):
    placed = (
        P(("replica", "row"), "col", None),
        P(("replica", "row"), "col", None),
        P("replica"),
        P(),
        P(),
        P(),
        P(),
        P(),
    )
    return jax.shard_map(
        step,
        mesh=mesh,
        in_specs=placed,
        out_specs=(P(("replica", "row"), "col", None), P(("replica", "row"), "col", None)),
        check_vma=False,
    )
```

```python
import functools

import jax
import jax.numpy as jnp
from jax import lax
from jax.experimental import pallas as pl
from jax.experimental.pallas import tpu as pltpu
from jax.sharding import PartitionSpec as P

eps_norm = 1e-05


def layer_norm(values, gain):
    mean_val = jnp.mean(values, axis=-1, keepdims=True)
    centred = values - mean_val
    inv_std = lax.rsqrt(jnp.mean(centred * centred, axis=-1, keepdims=True) + eps_norm)
    unit = centred * inv_std
    return (unit * gain, unit, inv_std)


def norm_back(grad_unit, unit, inv_std):
    first = jnp.mean(grad_unit, axis=-1, keepdims=True)
    second = jnp.mean(grad_unit * unit, axis=-1, keepdims=True)
    return inv_std * (grad_unit - first - unit * second)


def on_device(pair, cotangent, valid, in_gain, proj_weight, gate_weight, out_gain, out_weight):
    tile_rows = pair.shape[0]
    channels = pair.shape[2]
    hidden = out_weight.shape[0]
    cells = tile_rows * tile_rows
    keeper = valid.astype(jnp.float32)
    row_keep = lax.dynamic_slice_in_dim(keeper, lax.axis_index("row") * tile_rows, tile_rows)
    col_keep = lax.dynamic_slice_in_dim(keeper, lax.axis_index("col") * tile_rows, tile_rows)
    pair_keep = (row_keep[:, None] * col_keep[None, :])[:, :, None]
    normed_f, unit_in, inv_in = layer_norm(pair.astype(jnp.float32), in_gain)
    normed = normed_f.astype(jnp.bfloat16)
    flat = normed.reshape(cells, channels)
    proj = jnp.dot(flat, proj_weight, preferred_element_type=jnp.float32).reshape(
        tile_rows, tile_rows, 4 * hidden
    )
    left_sig = jax.nn.sigmoid(proj[..., :hidden])
    left_val = proj[..., hidden : 2 * hidden]
    right_sig = jax.nn.sigmoid(proj[..., 2 * hidden : 3 * hidden])
    right_val = proj[..., 3 * hidden :]
    left = (left_sig * left_val * pair_keep).astype(jnp.bfloat16)
    right = (right_sig * right_val * pair_keep).astype(jnp.bfloat16)
    panel = lax.all_gather(right, "row", axis=0, tiled=True)
    piece = panel
    tri = jnp.swapaxes(
        lax.psum_scatter(
            jnp.einsum("ikh,jkh->jih", left, piece, preferred_element_type=jnp.float32),
            "col",
            scatter_dimension=0,
            tiled=True,
        ),
        0,
        1,
    )
    tnorm_f, unit_tri, inv_tri = layer_norm(tri, out_gain)
    tnorm = tnorm_f.astype(jnp.bfloat16)
    gate = jax.nn.sigmoid(jnp.dot(flat, gate_weight, preferred_element_type=jnp.float32)).reshape(
        tile_rows, tile_rows, channels
    )
    lin = jnp.dot(
        tnorm.reshape(cells, hidden), out_weight, preferred_element_type=jnp.float32
    ).reshape(tile_rows, tile_rows, channels)
    update = (gate * lin).astype(jnp.bfloat16)
    cot = cotangent.astype(jnp.float32)
    d_lin = (cot * gate).astype(jnp.bfloat16)
    d_gpre = (cot * lin * gate * (1.0 - gate)).astype(jnp.bfloat16)
    d_tnorm = jnp.dot(
        d_lin.reshape(cells, channels), out_weight.T, preferred_element_type=jnp.float32
    ).reshape(tile_rows, tile_rows, hidden)
    d_tri = norm_back(d_tnorm * out_gain, unit_tri, inv_tri).astype(jnp.bfloat16)
    grad_rows = lax.all_gather(d_tri, "col", axis=1, tiled=True)
    back_panel = lax.all_gather(right, "row", axis=0, tiled=True)
    piece = grad_rows
    d_right = lax.psum_scatter(
        jnp.einsum("ijh,ikh->jkh", piece, left, preferred_element_type=jnp.float32),
        "row",
        scatter_dimension=0,
        tiled=True,
    )
    d_left = jnp.einsum("ijh,jkh->ikh", grad_rows, back_panel, preferred_element_type=jnp.float32)
    d_proj = jnp.concatenate(
        [
            d_left * pair_keep * left_val * left_sig * (1.0 - left_sig),
            d_left * pair_keep * left_sig,
            d_right * pair_keep * right_val * right_sig * (1.0 - right_sig),
            d_right * pair_keep * right_sig,
        ],
        axis=-1,
    ).astype(jnp.bfloat16)
    d_normed = jnp.dot(
        d_proj.reshape(cells, 4 * hidden), proj_weight.T, preferred_element_type=jnp.float32
    )
    d_normed = d_normed + jnp.dot(
        d_gpre.reshape(cells, channels), gate_weight.T, preferred_element_type=jnp.float32
    )
    pair_grad = norm_back(
        d_normed.reshape(tile_rows, tile_rows, channels) * in_gain, unit_in, inv_in
    )
    return (update, pair_grad)


F32 = jnp.float32
BF16 = jnp.bfloat16
LANES = 128
FIRST = (14, 15, 3, 12, 4, 10, 11, 13, 6, 0, 9, 2, 1, 5, 8, 7)
LATER = (6, 7, 11, 0, 12, 2, 3, 5, 14, 8, 1, 10, 9, 13, 4, 15)
FIRST_PLACE = tuple(FIRST.index(device) for device in range(len(FIRST)))
LATER_PLACE = tuple(LATER.index(device) for device in range(len(LATER)))
HOLDER = tuple(LATER.index(device) for device in FIRST)


def dot(a, b, dims):
    return lax.dot_general(a, b, ((dims[:1], dims[1:]), ((), ())), preferred_element_type=F32)


def column(gain):
    n = gain.shape[1]
    return jnp.broadcast_to(gain, (n, n)).T


def spread(col, width):
    return jnp.concatenate([col] * (width // col.shape[1]), axis=1)


def unit_rows(values):
    n = values.shape[0]
    centred = values - jnp.sum(values, axis=0, keepdims=True) * (1.0 / n)
    inv = lax.rsqrt(jnp.sum(centred * centred, axis=0, keepdims=True) * (1.0 / n) + eps_norm)
    return centred * inv, inv


def unit_back(q, unit, inv):
    n = q.shape[0]
    first = jnp.sum(q, axis=0, keepdims=True) * (1.0 / n)
    second = jnp.sum(q * unit, axis=0, keepdims=True) * (1.0 / n)
    return inv * (q - first - unit * second)


def one_hot(at):
    return jnp.where(at, 1.0, 0.0).astype(BF16)


def block_swap():
    width = LANES // 4
    row = lax.broadcasted_iota(jnp.int32, (width, LANES), 0)
    lane = lax.broadcasted_iota(jnp.int32, (width, LANES), 1)
    none = jnp.zeros((width, LANES), BF16)
    to = [one_hot(row + width * c == lane) for c in range(4)]
    return jnp.concatenate(
        [jnp.concatenate([to[c] if n == p else none for n in range(4)], axis=1) for c in range(4) for p in range(4)],
        axis=0,
    )


def keep_row(valid, tile, cells):
    n = valid.ref.shape[1]
    groups, rows = cells // n, n // tile
    token = lax.broadcasted_iota(jnp.int32, (n, n), 0)
    lane = lax.broadcasted_iota(jnp.int32, (n, n), 1)
    place = lax.broadcasted_iota(jnp.int32, (groups, n), 1) - lax.axis_index("row") * tile
    group = rows * lax.broadcasted_iota(jnp.int32, (groups, n), 0)
    inside = jnp.logical_and(place >= group, place < group + rows)
    first = one_hot(lax.rem(token, rows) == lax.div(lane, tile))
    second = one_hot(token - lax.axis_index("col") * tile == lax.rem(lane, tile))
    v = jnp.broadcast_to(valid.ready()[...].astype(F32), (groups, n))
    own = jnp.where(inside, v, 0.0).astype(BF16)
    keep = dot(own, first, (1, 0)) * dot(v.astype(BF16), second, (1, 0))
    return jnp.concatenate([keep[g : g + 1] for g in range(groups)], axis=1)


def normed_of(pair, in_gain):
    unit, inv = unit_rows(pair.ready()[...].astype(F32).T)
    normed = (unit * spread(column(in_gain.ready()[...]), unit.shape[1])).astype(BF16)
    return normed, unit, inv


def project_kernel(tile, parts, pair, proj_weight, valid, in_gain, out):
    cells, channels = pair.ref.shape
    hidden = proj_weight.ref.shape[1] // 4
    shards, both, _ = out.ref.shape
    per = both // 2
    keep = keep_row(valid, tile, cells)
    normed, _, _ = normed_of(pair, in_gain)
    weights = proj_weight.ready()[...].T
    share = hidden // parts
    for part in range(parts):
        rows = [weights[block * hidden + part * share : block * hidden + (part + 1) * share] for block in range(4)]
        proj = dot(jnp.concatenate(rows, axis=0), normed, (1, 0))
        left = jax.nn.sigmoid(proj[:share]) * proj[share : 2 * share] * keep
        right = jax.nn.sigmoid(proj[2 * share : 3 * share]) * proj[3 * share :] * keep
        for s in range(shards // parts):
            own = slice(s * per, (s + 1) * per)
            out.ref[part * shards // parts + s] = jnp.concatenate([left[own], right[own]], axis=0).astype(BF16)
        out.send(part)


def gate_of(normed, cot, gate_weight):
    gate = jax.nn.sigmoid(dot(gate_weight.ready()[...].T, normed, (1, 0)))
    return gate, cot.ready()[...].astype(F32).T


def gate_kernel(pair, cot, in_gain, gate_weight, out_gain, out_weight, q_ref):
    normed, _, _ = normed_of(pair, in_gain)
    gate, cot_rows = gate_of(normed, cot, gate_weight)
    q = dot(out_weight.ready()[...], (cot_rows * gate).astype(BF16), (1, 0))
    q_ref[...] = q * spread(column(out_gain.ready()[...]), q.shape[1])


def tri_kernel(grid_rows, recv_ref, out_ref, left_ref, right_ref, rows, tri):
    devices, both, cells = recv_ref.shape
    per = both // 2
    n = left_ref.shape[1]
    tile = n // grid_rows
    groups = cells // LANES
    swap = block_swap()
    for r in range(grid_rows):
        x = jnp.concatenate(
            [
                jnp.concatenate(
                    [recv_ref[FIRST_PLACE[grid_rows * r + c], :, g * LANES : (g + 1) * LANES] for c in range(grid_rows)], axis=1
                )
                for g in range(groups)
            ],
            axis=0,
        )
        y = dot(x, swap, (1, 0))
        for g in range(groups):
            for p in range(grid_rows):
                at = (r * tile + g * grid_rows + p) * both
                rows[at : at + both, :] = y[g * both : (g + 1) * both, p * LANES : (p + 1) * LANES]
    for h in range(per):
        left = rows[pl.ds(h, n, stride=both), :].astype(BF16)
        right = rows[pl.ds(per + h, n, stride=both), :].astype(BF16)
        left_ref[h] = left
        right_ref[h] = right
        tri[pl.ds(h, n, stride=per), :] = dot(left, right, (1, 1))
    half = groups // 2
    for r in range(grid_rows):
        x = jnp.concatenate(
            [
                jnp.concatenate(
                    [
                        tri[at : at + per, :]
                        for p in range(grid_rows)
                        for at in [(r * tile + (g + k * half) * grid_rows + p) * per]
                    ],
                    axis=1,
                )
                for g in range(half)
                for k in range(2)
            ],
            axis=0,
        )
        y = dot(x.astype(BF16), swap, (1, 0)).astype(BF16)
        for g in range(half):
            for c in range(grid_rows):
                out_ref[LATER_PLACE[grid_rows * r + c], :, g * LANES : (g + 1) * LANES] = y[
                    g * both : (g + 1) * both, c * LANES : (c + 1) * LANES
                ]


def halves_of(recv_ref):
    per = recv_ref.shape[1] // 2
    blocks = [recv_ref[holder].astype(F32) for holder in HOLDER]
    return jnp.concatenate(
        [jnp.concatenate([b[k * per : (k + 1) * per] for b in blocks], axis=0) for k in range(2)], axis=1
    )


def d_tri_kernel(recv_ref, q_ref, out_ref):
    _, both, width = recv_ref.shape
    per = both // 2
    unit, inv = unit_rows(halves_of(recv_ref))
    d_tri = unit_back(q_ref[...], unit, inv)
    for shard, holder in enumerate(HOLDER):
        rows = d_tri[shard * per : (shard + 1) * per]
        out_ref[holder] = jnp.concatenate([rows[:, :width], rows[:, width:]], axis=0).astype(BF16)


def update_kernel(
    tile, tri, out_gain, out_weight, pair, cot, valid, in_gain, gate_weight, proj_weight,
    unit_ref, inv_ref, factor_ref, update,
):
    normed, unit, inv = normed_of(pair, in_gain)
    unit_ref[...] = unit
    inv_ref[...] = inv
    gate, cot_rows = gate_of(normed, cot, gate_weight)
    unit_tri, _ = unit_rows(halves_of(tri.ready()))
    tnorm = (unit_tri * spread(column(out_gain.ready()[...]), unit.shape[1])).astype(BF16)
    lin = dot(out_weight.ready()[...].T, tnorm, (1, 0))
    update.ref[...] = (gate * lin).T.astype(BF16)
    update.send()
    factor_ref[4] = (cot_rows * lin * gate * (1.0 - gate)).astype(BF16)
    hidden = proj_weight.ref.shape[1] // 4
    keep = keep_row(valid, tile, unit.shape[1])
    weights = proj_weight.ready()
    for side in range(2):
        weight = weights[:, 2 * hidden * side : 2 * hidden * (side + 1)].T
        proj = dot(weight, normed, (1, 0))
        sig = jax.nn.sigmoid(proj[:hidden])
        factor_ref[2 * side] = (keep * proj[hidden:] * sig * (1.0 - sig)).astype(BF16)
        factor_ref[2 * side + 1] = (keep * sig).astype(BF16)


def sides_kernel(grid_rows, recv_ref, left_ref, right_ref, out, d_tri, rows):
    devices, both, cells = out.ref.shape
    per = both // 2
    n = left_ref.shape[1]
    tile = n // grid_rows
    groups = cells // LANES
    half = groups // 2
    swap = block_swap()
    for r in range(grid_rows):
        x = jnp.concatenate(
            [
                jnp.concatenate(
                    [recv_ref[LATER_PLACE[grid_rows * r + c], :, g * LANES : (g + 1) * LANES] for c in range(grid_rows)], axis=1
                )
                for g in range(half)
            ],
            axis=0,
        )
        y = dot(x, swap, (1, 0))
        for g in range(half):
            for k in range(2):
                for p in range(grid_rows):
                    at = (r * tile + (g + k * half) * grid_rows + p) * per
                    d_tri[at : at + per, :] = y[
                        g * both + k * per : g * both + (k + 1) * per, p * LANES : (p + 1) * LANES
                    ]
    for h in range(per):
        grad = d_tri[pl.ds(h, n, stride=per), :].astype(BF16)
        rows[pl.ds(h, n, stride=both), :] = dot(grad, right_ref[h], (1, 0))
        rows[pl.ds(per + h, n, stride=both), :] = dot(grad, left_ref[h], (0, 0))
    for r in range(grid_rows):
        x = jnp.concatenate(
            [
                jnp.concatenate(
                    [
                        rows[at : at + both, :]
                        for p in range(grid_rows)
                        for at in [(r * tile + g * grid_rows + p) * both]
                    ],
                    axis=1,
                )
                for g in range(groups)
            ],
            axis=0,
        )
        y = dot(x.astype(BF16), swap, (1, 0)).astype(BF16)
        for c in range(grid_rows):
            place = LATER_PLACE[grid_rows * r + c]
            for g in range(groups):
                out.ref[place, :, g * LANES : (g + 1) * LANES] = y[
                    g * both : (g + 1) * both, c * LANES : (c + 1) * LANES
                ]
            out.send(place)


def pair_grad_kernel(parts, recv_ref, factor_ref, unit_ref, inv_ref, in_gain, proj_weight, gate_weight, out):
    _, both, cells = recv_ref.shape
    width = cells // parts
    gain = spread(column(in_gain.ready()[...]), width)
    weights, gate_weights = proj_weight.ready()[...], gate_weight.ready()[...]
    for part in range(parts):
        lanes = slice(part * width, (part + 1) * width)
        blocks = [recv_ref[holder, :, lanes].astype(F32) for holder in HOLDER]
        grads = [
            jnp.concatenate([b[k * both // 2 : (k + 1) * both // 2] for b in blocks], axis=0) for k in range(2)
        ]
        d_proj = jnp.concatenate(
            [
                (grad * factor_ref[2 * side + k, :, lanes].astype(F32)).astype(BF16)
                for side, grad in enumerate(grads)
                for k in range(2)
            ],
            axis=0,
        )
        d_normed = dot(weights, d_proj, (1, 0)) + dot(gate_weights, factor_ref[4, :, lanes], (1, 0))
        out.ref[lanes, :] = unit_back(d_normed * gain, unit_ref[:, lanes], inv_ref[:, lanes]).T
        out.send(part)


class Arriving:
    def __init__(self, source, ref, sems, parts):
        size = ref.shape[0] // parts
        cuts = [pl.ds(part * size, size) for part in range(parts)]
        self.ref = ref
        self.copies = [pltpu.make_async_copy(source.at[cut], ref.at[cut], sem) for cut, sem in zip(cuts, sems)]
        for copy in self.copies:
            copy.start()
        self.waiting = set(range(parts))

    def ready(self, part=None):
        for one in sorted(self.waiting) if part is None else [part]:
            if one in self.waiting:
                self.copies[one].wait()
                self.waiting.remove(one)
        return self.ref


class Leaving:
    def __init__(self, target, ref, sems, parts, dim):
        size = ref.shape[dim] // parts
        cuts = [(slice(None),) * dim + (pl.ds(part * size, size),) for part in range(parts)]
        self.ref = ref
        self.copies = [pltpu.make_async_copy(ref.at[cut], target.at[cut], sem) for cut, sem in zip(cuts, sems)]

    def send(self, part=0):
        self.copies[part].start()


def call(kernel, outs, args, flops, scratch=(), far=(), far_outs=(), room=24):
    outs, args, scratch = list(outs), list(args), list(scratch)
    far = [one if isinstance(one, tuple) else (one, 1) for one in far]
    far_outs = [one if isinstance(one, tuple) else (one, 1, 0) for one in far_outs]
    far_arrays, far_shapes = [one[0] for one in far], [one[0] for one in far_outs]
    counts = [len(args), len(far), len(outs), len(far_outs), len(far), len(far_outs), len(scratch)]

    def body(*refs):
        groups, at = [], 0
        for count in counts:
            groups.append(list(refs[at : at + count]))
            at += count
        near_in, far_in, near_out, far_out, held, leaving, rest = groups
        sems = refs[at]
        used = 0
        arrivals, departures = [], []
        for source, ref, (_, parts) in zip(far_in, held, far):
            arrivals.append(Arriving(source, ref, [sems.at[used + k] for k in range(parts)], parts))
            used += parts
        for target, ref, (_, parts, dim) in zip(far_out, leaving, far_outs):
            departures.append(Leaving(target, ref, [sems.at[used + k] for k in range(parts)], parts, dim))
            used += parts
        kernel(*near_in, *arrivals, *near_out, *departures, *rest)
        for one in arrivals:
            one.ready()
        for one in departures:
            for copy in one.copies:
                copy.wait()

    near_spec, far_spec = pl.BlockSpec(memory_space=pltpu.VMEM), pl.BlockSpec(memory_space=pltpu.HBM)
    moved = sum(a.size * a.dtype.itemsize for a in args + far_arrays + outs + far_shapes)
    return pl.pallas_call(
        body,
        out_shape=tuple(outs + far_shapes),
        in_specs=[near_spec] * len(args) + [far_spec] * len(far),
        out_specs=tuple([near_spec] * len(outs) + [far_spec] * len(far_outs)),
        scratch_shapes=[pltpu.VMEM(a.shape, a.dtype) for a in far_arrays + far_shapes]
        + scratch
        + [pltpu.SemaphoreType.DMA((max(1, sum(one[1] for one in far + far_outs)),))],
        compiler_params=pltpu.CompilerParams(vmem_limit_bytes=int(room * 2**20)),
        cost_estimate=pl.CostEstimate(flops=flops, bytes_accessed=moved, transcendentals=0),
    )(*args, *far_arrays)


def by_channel(pair, cotangent, valid, in_gain, proj_weight, gate_weight, out_gain, out_weight):
    tile, _, channels = pair.shape
    hidden = out_weight.shape[0]
    cells = tile * tile
    grid_rows = lax.axis_size("row")
    devices = grid_rows * lax.axis_size("col")
    per = hidden // devices
    n = tile * grid_rows
    shape = lambda dims, dtype: jax.ShapeDtypeStruct(dims, dtype)
    exchange = lambda x, order: lax.all_to_all(x, ("row", "col"), 0, 0, axis_index_groups=[order], tiled=True)
    flat = pair.reshape(cells, channels)
    flat_cot = cotangent.reshape(cells, channels)
    valid_row = valid.reshape(1, -1)
    in_row = in_gain.reshape(1, -1)
    out_row = out_gain.reshape(1, -1)
    both = 2 * per
    plane = shape((channels, cells), F32)

    (sides,) = call(
        functools.partial(project_kernel, tile, 4),
        [],
        (),
        2 * cells * channels * 4 * hidden,
        far=(flat, proj_weight, valid_row, in_row),
        far_outs=[(shape((devices, both, cells), BF16), 4, 0)],
        room=62,
    )
    sides, flat_2, flat_cot_2 = lax.optimization_barrier((sides, flat, flat_cot))
    sides = exchange(sides, FIRST)
    (q,) = call(
        gate_kernel,
        [plane],
        (),
        2 * cells * channels * 2 * hidden,
        far=(flat_2, flat_cot_2, in_row, gate_weight, out_row, out_weight),
    )
    sides, q = lax.optimization_barrier((sides, q))
    tri, left, right = call(
        functools.partial(tri_kernel, grid_rows),
        [shape((devices, both, cells // 2), BF16), shape((per, n, n), BF16), shape((per, n, n), BF16)],
        (sides,),
        2 * per * n * n * n,
        [pltpu.VMEM((n * both, n), F32), pltpu.VMEM((n * per, n), F32)],
    )
    tri = exchange(tri, LATER)
    (d_tri,) = call(
        d_tri_kernel,
        [shape((devices, both, cells // 2), BF16)],
        (tri, q),
        20 * cells * hidden,
    )
    d_tri = exchange(d_tri, LATER)
    (d_sides,) = call(
        functools.partial(sides_kernel, grid_rows),
        [],
        (d_tri, left, right),
        4 * per * n * n * n,
        [pltpu.VMEM((n * per, n), F32), pltpu.VMEM((n * both, n), F32)],
        far_outs=[(shape((devices, both, cells), BF16), devices, 0)],
    )
    d_sides, flat_4, flat_cot_4, tri = lax.optimization_barrier((d_sides, flat, flat_cot, tri))
    d_sides = exchange(d_sides, LATER)
    unit, inv, factors, update = call(
        functools.partial(update_kernel, tile),
        [plane, shape((1, cells), F32), shape((5, hidden, cells), BF16)],
        (),
        2 * cells * channels * 6 * hidden,
        far=(tri, out_row, out_weight, flat_4, flat_cot_4, valid_row, in_row, gate_weight, proj_weight),
        far_outs=[shape((cells, channels), BF16)],
    )
    (pair_grad,) = call(
        functools.partial(pair_grad_kernel, 4),
        [],
        (d_sides, factors, unit, inv),
        2 * cells * channels * 5 * hidden,
        far=(in_row, proj_weight, gate_weight),
        far_outs=[(shape((cells, channels), F32), 4, 0)],
    )
    return (update.reshape(pair.shape), pair_grad.reshape(pair.shape))


def fits(pair, out_weight):
    rows, cols = lax.axis_size("row"), lax.axis_size("col")
    tile, tile_cols, channels = pair.shape
    hidden = out_weight.shape[0]
    return (
        rows == cols == 4
        and tile == tile_cols
        and tile * rows == LANES
        and channels == LANES
        and hidden == 8 * rows * cols
    )


def step(pair, cotangent, valid, in_gain, proj_weight, gate_weight, out_gain, out_weight):
    plan = by_channel if fits(pair, out_weight) else on_device
    return plan(pair, cotangent, valid, in_gain, proj_weight, gate_weight, out_gain, out_weight)


def solution(mesh):
    placed = (
        P(("replica", "row"), "col", None),
        P(("replica", "row"), "col", None),
        P("replica"),
        P(),
        P(),
        P(),
        P(),
        P(),
    )
    return jax.shard_map(
        step,
        mesh=mesh,
        in_specs=placed,
        out_specs=(P(("replica", "row"), "col", None), P(("replica", "row"), "col", None)),
        check_vma=False,
    )
```

```python
import functools

import jax
import jax.numpy as jnp
from jax import lax
from jax.experimental import pallas as pl
from jax.experimental.pallas import tpu as pltpu
from jax.sharding import PartitionSpec as P

eps_norm = 1e-05


def layer_norm(values, gain):
    mean_val = jnp.mean(values, axis=-1, keepdims=True)
    centred = values - mean_val
    inv_std = lax.rsqrt(jnp.mean(centred * centred, axis=-1, keepdims=True) + eps_norm)
    unit = centred * inv_std
    return (unit * gain, unit, inv_std)


def norm_back(grad_unit, unit, inv_std):
    first = jnp.mean(grad_unit, axis=-1, keepdims=True)
    second = jnp.mean(grad_unit * unit, axis=-1, keepdims=True)
    return inv_std * (grad_unit - first - unit * second)


def on_device(pair, cotangent, valid, in_gain, proj_weight, gate_weight, out_gain, out_weight):
    tile_rows = pair.shape[0]
    channels = pair.shape[2]
    hidden = out_weight.shape[0]
    cells = tile_rows * tile_rows
    keeper = valid.astype(jnp.float32)
    row_keep = lax.dynamic_slice_in_dim(keeper, lax.axis_index("row") * tile_rows, tile_rows)
    col_keep = lax.dynamic_slice_in_dim(keeper, lax.axis_index("col") * tile_rows, tile_rows)
    pair_keep = (row_keep[:, None] * col_keep[None, :])[:, :, None]
    normed_f, unit_in, inv_in = layer_norm(pair.astype(jnp.float32), in_gain)
    normed = normed_f.astype(jnp.bfloat16)
    flat = normed.reshape(cells, channels)
    proj = jnp.dot(flat, proj_weight, preferred_element_type=jnp.float32).reshape(
        tile_rows, tile_rows, 4 * hidden
    )
    left_sig = jax.nn.sigmoid(proj[..., :hidden])
    left_val = proj[..., hidden : 2 * hidden]
    right_sig = jax.nn.sigmoid(proj[..., 2 * hidden : 3 * hidden])
    right_val = proj[..., 3 * hidden :]
    left = (left_sig * left_val * pair_keep).astype(jnp.bfloat16)
    right = (right_sig * right_val * pair_keep).astype(jnp.bfloat16)
    panel = lax.all_gather(right, "row", axis=0, tiled=True)
    piece = panel
    tri = jnp.swapaxes(
        lax.psum_scatter(
            jnp.einsum("ikh,jkh->jih", left, piece, preferred_element_type=jnp.float32),
            "col",
            scatter_dimension=0,
            tiled=True,
        ),
        0,
        1,
    )
    tnorm_f, unit_tri, inv_tri = layer_norm(tri, out_gain)
    tnorm = tnorm_f.astype(jnp.bfloat16)
    gate = jax.nn.sigmoid(jnp.dot(flat, gate_weight, preferred_element_type=jnp.float32)).reshape(
        tile_rows, tile_rows, channels
    )
    lin = jnp.dot(
        tnorm.reshape(cells, hidden), out_weight, preferred_element_type=jnp.float32
    ).reshape(tile_rows, tile_rows, channels)
    update = (gate * lin).astype(jnp.bfloat16)
    cot = cotangent.astype(jnp.float32)
    d_lin = (cot * gate).astype(jnp.bfloat16)
    d_gpre = (cot * lin * gate * (1.0 - gate)).astype(jnp.bfloat16)
    d_tnorm = jnp.dot(
        d_lin.reshape(cells, channels), out_weight.T, preferred_element_type=jnp.float32
    ).reshape(tile_rows, tile_rows, hidden)
    d_tri = norm_back(d_tnorm * out_gain, unit_tri, inv_tri).astype(jnp.bfloat16)
    grad_rows = lax.all_gather(d_tri, "col", axis=1, tiled=True)
    back_panel = lax.all_gather(right, "row", axis=0, tiled=True)
    piece = grad_rows
    d_right = lax.psum_scatter(
        jnp.einsum("ijh,ikh->jkh", piece, left, preferred_element_type=jnp.float32),
        "row",
        scatter_dimension=0,
        tiled=True,
    )
    d_left = jnp.einsum("ijh,jkh->ikh", grad_rows, back_panel, preferred_element_type=jnp.float32)
    d_proj = jnp.concatenate(
        [
            d_left * pair_keep * left_val * left_sig * (1.0 - left_sig),
            d_left * pair_keep * left_sig,
            d_right * pair_keep * right_val * right_sig * (1.0 - right_sig),
            d_right * pair_keep * right_sig,
        ],
        axis=-1,
    ).astype(jnp.bfloat16)
    d_normed = jnp.dot(
        d_proj.reshape(cells, 4 * hidden), proj_weight.T, preferred_element_type=jnp.float32
    )
    d_normed = d_normed + jnp.dot(
        d_gpre.reshape(cells, channels), gate_weight.T, preferred_element_type=jnp.float32
    )
    pair_grad = norm_back(
        d_normed.reshape(tile_rows, tile_rows, channels) * in_gain, unit_in, inv_in
    )
    return (update, pair_grad)


F32 = jnp.float32
BF16 = jnp.bfloat16
LANES = 128
FIRST = (14, 15, 3, 12, 4, 10, 11, 13, 6, 0, 9, 2, 1, 5, 8, 7)
LATER = (14, 15, 3, 4, 13, 10, 11, 12, 6, 0, 9, 2, 1, 5, 8, 7)
FIRST_PLACE = tuple(FIRST.index(device) for device in range(len(FIRST)))
LATER_PLACE = tuple(LATER.index(device) for device in range(len(LATER)))
HOLDER = tuple(LATER.index(device) for device in FIRST)


def dot(a, b, dims):
    return lax.dot_general(a, b, ((dims[:1], dims[1:]), ((), ())), preferred_element_type=F32)


def column(gain):
    n = gain.shape[1]
    return jnp.broadcast_to(gain, (n, n)).T


def spread(col, width):
    return jnp.concatenate([col] * (width // col.shape[1]), axis=1)


def unit_rows(values):
    n = values.shape[0]
    centred = values - jnp.sum(values, axis=0, keepdims=True) * (1.0 / n)
    inv = lax.rsqrt(jnp.sum(centred * centred, axis=0, keepdims=True) * (1.0 / n) + eps_norm)
    return centred * inv, inv


def unit_back(q, unit, inv):
    n = q.shape[0]
    first = jnp.sum(q, axis=0, keepdims=True) * (1.0 / n)
    second = jnp.sum(q * unit, axis=0, keepdims=True) * (1.0 / n)
    return inv * (q - first - unit * second)


def one_hot(at):
    return jnp.where(at, 1.0, 0.0).astype(BF16)


def block_swap():
    width = LANES // 4
    row = lax.broadcasted_iota(jnp.int32, (width, LANES), 0)
    lane = lax.broadcasted_iota(jnp.int32, (width, LANES), 1)
    none = jnp.zeros((width, LANES), BF16)
    to = [one_hot(row + width * c == lane) for c in range(4)]
    return jnp.concatenate(
        [jnp.concatenate([to[c] if n == p else none for n in range(4)], axis=1) for c in range(4) for p in range(4)],
        axis=0,
    )


def keep_row(valid, tile, cells):
    n = valid.ref.shape[1]
    groups, rows = cells // n, n // tile
    token = lax.broadcasted_iota(jnp.int32, (n, n), 0)
    lane = lax.broadcasted_iota(jnp.int32, (n, n), 1)
    place = lax.broadcasted_iota(jnp.int32, (groups, n), 1) - lax.axis_index("row") * tile
    group = rows * lax.broadcasted_iota(jnp.int32, (groups, n), 0)
    inside = jnp.logical_and(place >= group, place < group + rows)
    first = one_hot(lax.rem(token, rows) == lax.div(lane, tile))
    second = one_hot(token - lax.axis_index("col") * tile == lax.rem(lane, tile))
    v = jnp.broadcast_to(valid.ready()[...].astype(F32), (groups, n))
    own = jnp.where(inside, v, 0.0).astype(BF16)
    keep = dot(own, first, (1, 0)) * dot(v.astype(BF16), second, (1, 0))
    return jnp.concatenate([keep[g : g + 1] for g in range(groups)], axis=1)


def normed_of(pair, in_gain):
    unit, inv = unit_rows(pair.ready()[...].astype(F32).T)
    normed = (unit * spread(column(in_gain.ready()[...]), unit.shape[1])).astype(BF16)
    return normed, unit, inv


def project_kernel(tile, parts, pair, proj_weight, valid, in_gain, out):
    cells, channels = pair.ref.shape
    hidden = proj_weight.ref.shape[1] // 4
    shards, both, _ = out.ref.shape
    per = both // 2
    keep = keep_row(valid, tile, cells)
    normed, _, _ = normed_of(pair, in_gain)
    weights = proj_weight.ready()[...].T
    share = hidden // parts
    for part in range(parts):
        rows = [weights[block * hidden + part * share : block * hidden + (part + 1) * share] for block in range(4)]
        proj = dot(jnp.concatenate(rows, axis=0), normed, (1, 0))
        left = jax.nn.sigmoid(proj[:share]) * proj[share : 2 * share] * keep
        right = jax.nn.sigmoid(proj[2 * share : 3 * share]) * proj[3 * share :] * keep
        for s in range(shards // parts):
            own = slice(s * per, (s + 1) * per)
            out.ref[part * shards // parts + s] = jnp.concatenate([left[own], right[own]], axis=0).astype(BF16)
        out.send(part)


def gate_of(normed, cot, gate_weight):
    gate = jax.nn.sigmoid(dot(gate_weight.ready()[...].T, normed, (1, 0)))
    return gate, cot.ready()[...].astype(F32).T


def gate_kernel(pair, cot, in_gain, gate_weight, out_gain, out_weight, q_ref):
    normed, _, _ = normed_of(pair, in_gain)
    gate, cot_rows = gate_of(normed, cot, gate_weight)
    q = dot(out_weight.ready()[...], (cot_rows * gate).astype(BF16), (1, 0))
    q_ref[...] = q * spread(column(out_gain.ready()[...]), q.shape[1])


def tri_kernel(grid_rows, recv_ref, out_ref, left_ref, right_ref, rows, tri):
    devices, both, cells = recv_ref.shape
    per = both // 2
    n = left_ref.shape[1]
    tile = n // grid_rows
    groups = cells // LANES
    swap = block_swap()
    for r in range(grid_rows):
        x = jnp.concatenate(
            [
                jnp.concatenate(
                    [recv_ref[FIRST_PLACE[grid_rows * r + c], :, g * LANES : (g + 1) * LANES] for c in range(grid_rows)], axis=1
                )
                for g in range(groups)
            ],
            axis=0,
        )
        y = dot(x, swap, (1, 0))
        for g in range(groups):
            for p in range(grid_rows):
                at = (r * tile + g * grid_rows + p) * both
                rows[at : at + both, :] = y[g * both : (g + 1) * both, p * LANES : (p + 1) * LANES]
    for h in range(per):
        left = rows[pl.ds(h, n, stride=both), :].astype(BF16)
        right = rows[pl.ds(per + h, n, stride=both), :].astype(BF16)
        left_ref[h] = left
        right_ref[h] = right
        tri[pl.ds(h, n, stride=per), :] = dot(left, right, (1, 1))
    half = groups // 2
    for r in range(grid_rows):
        x = jnp.concatenate(
            [
                jnp.concatenate(
                    [
                        tri[at : at + per, :]
                        for p in range(grid_rows)
                        for at in [(r * tile + (g + k * half) * grid_rows + p) * per]
                    ],
                    axis=1,
                )
                for g in range(half)
                for k in range(2)
            ],
            axis=0,
        )
        y = dot(x.astype(BF16), swap, (1, 0)).astype(BF16)
        for g in range(half):
            for c in range(grid_rows):
                out_ref[LATER_PLACE[grid_rows * r + c], :, g * LANES : (g + 1) * LANES] = y[
                    g * both : (g + 1) * both, c * LANES : (c + 1) * LANES
                ]


def halves_of(recv_ref):
    per = recv_ref.shape[1] // 2
    blocks = [recv_ref[holder].astype(F32) for holder in HOLDER]
    return jnp.concatenate(
        [jnp.concatenate([b[k * per : (k + 1) * per] for b in blocks], axis=0) for k in range(2)], axis=1
    )


def d_tri_kernel(recv_ref, q_ref, out_ref):
    _, both, width = recv_ref.shape
    per = both // 2
    unit, inv = unit_rows(halves_of(recv_ref))
    d_tri = unit_back(q_ref[...], unit, inv)
    for shard, holder in enumerate(HOLDER):
        rows = d_tri[shard * per : (shard + 1) * per]
        out_ref[holder] = jnp.concatenate([rows[:, :width], rows[:, width:]], axis=0).astype(BF16)


def update_kernel(
    tile, tri, out_gain, out_weight, pair, cot, valid, in_gain, gate_weight, proj_weight,
    unit_ref, inv_ref, factor_ref, update,
):
    normed, unit, inv = normed_of(pair, in_gain)
    unit_ref[...] = unit
    inv_ref[...] = inv
    gate, cot_rows = gate_of(normed, cot, gate_weight)
    unit_tri, _ = unit_rows(halves_of(tri.ready()))
    tnorm = (unit_tri * spread(column(out_gain.ready()[...]), unit.shape[1])).astype(BF16)
    lin = dot(out_weight.ready()[...].T, tnorm, (1, 0))
    update.ref[...] = (gate * lin).T.astype(BF16)
    update.send()
    factor_ref[4] = (cot_rows * lin * gate * (1.0 - gate)).astype(BF16)
    hidden = proj_weight.ref.shape[1] // 4
    keep = keep_row(valid, tile, unit.shape[1])
    weights = proj_weight.ready()
    for side in range(2):
        weight = weights[:, 2 * hidden * side : 2 * hidden * (side + 1)].T
        proj = dot(weight, normed, (1, 0))
        sig = jax.nn.sigmoid(proj[:hidden])
        factor_ref[2 * side] = (keep * proj[hidden:] * sig * (1.0 - sig)).astype(BF16)
        factor_ref[2 * side + 1] = (keep * sig).astype(BF16)


def sides_kernel(grid_rows, recv_ref, left_ref, right_ref, out, d_tri, rows):
    devices, both, cells = out.ref.shape
    per = both // 2
    n = left_ref.shape[1]
    tile = n // grid_rows
    groups = cells // LANES
    half = groups // 2
    swap = block_swap()
    for r in range(grid_rows):
        x = jnp.concatenate(
            [
                jnp.concatenate(
                    [recv_ref[LATER_PLACE[grid_rows * r + c], :, g * LANES : (g + 1) * LANES] for c in range(grid_rows)], axis=1
                )
                for g in range(half)
            ],
            axis=0,
        )
        y = dot(x, swap, (1, 0))
        for g in range(half):
            for k in range(2):
                for p in range(grid_rows):
                    at = (r * tile + (g + k * half) * grid_rows + p) * per
                    d_tri[at : at + per, :] = y[
                        g * both + k * per : g * both + (k + 1) * per, p * LANES : (p + 1) * LANES
                    ]
    for h in range(per):
        grad = d_tri[pl.ds(h, n, stride=per), :].astype(BF16)
        rows[pl.ds(h, n, stride=both), :] = dot(grad, right_ref[h], (1, 0))
        rows[pl.ds(per + h, n, stride=both), :] = dot(grad, left_ref[h], (0, 0))
    for r in range(grid_rows):
        x = jnp.concatenate(
            [
                jnp.concatenate(
                    [
                        rows[at : at + both, :]
                        for p in range(grid_rows)
                        for at in [(r * tile + g * grid_rows + p) * both]
                    ],
                    axis=1,
                )
                for g in range(groups)
            ],
            axis=0,
        )
        y = dot(x.astype(BF16), swap, (1, 0)).astype(BF16)
        for c in range(grid_rows):
            place = LATER_PLACE[grid_rows * r + c]
            for g in range(groups):
                out.ref[place, :, g * LANES : (g + 1) * LANES] = y[
                    g * both : (g + 1) * both, c * LANES : (c + 1) * LANES
                ]
            out.send(place)


def pair_grad_kernel(parts, recv_ref, factor_ref, unit_ref, inv_ref, in_gain, proj_weight, gate_weight, out):
    _, both, cells = recv_ref.shape
    width = cells // parts
    gain = spread(column(in_gain.ready()[...]), width)
    weights, gate_weights = proj_weight.ready()[...], gate_weight.ready()[...]
    for part in range(parts):
        lanes = slice(part * width, (part + 1) * width)
        blocks = [recv_ref[holder, :, lanes].astype(F32) for holder in HOLDER]
        grads = [
            jnp.concatenate([b[k * both // 2 : (k + 1) * both // 2] for b in blocks], axis=0) for k in range(2)
        ]
        d_proj = jnp.concatenate(
            [
                (grad * factor_ref[2 * side + k, :, lanes].astype(F32)).astype(BF16)
                for side, grad in enumerate(grads)
                for k in range(2)
            ],
            axis=0,
        )
        d_normed = dot(weights, d_proj, (1, 0)) + dot(gate_weights, factor_ref[4, :, lanes], (1, 0))
        out.ref[lanes, :] = unit_back(d_normed * gain, unit_ref[:, lanes], inv_ref[:, lanes]).T
        out.send(part)


class Arriving:
    def __init__(self, source, ref, sems, parts):
        size = ref.shape[0] // parts
        cuts = [pl.ds(part * size, size) for part in range(parts)]
        self.ref = ref
        self.copies = [pltpu.make_async_copy(source.at[cut], ref.at[cut], sem) for cut, sem in zip(cuts, sems)]
        for copy in self.copies:
            copy.start()
        self.waiting = set(range(parts))

    def ready(self, part=None):
        for one in sorted(self.waiting) if part is None else [part]:
            if one in self.waiting:
                self.copies[one].wait()
                self.waiting.remove(one)
        return self.ref


class Leaving:
    def __init__(self, target, ref, sems, parts, dim):
        size = ref.shape[dim] // parts
        cuts = [(slice(None),) * dim + (pl.ds(part * size, size),) for part in range(parts)]
        self.ref = ref
        self.copies = [pltpu.make_async_copy(ref.at[cut], target.at[cut], sem) for cut, sem in zip(cuts, sems)]

    def send(self, part=0):
        self.copies[part].start()


def call(kernel, outs, args, flops, scratch=(), far=(), far_outs=(), room=24):
    outs, args, scratch = list(outs), list(args), list(scratch)
    far = [one if isinstance(one, tuple) else (one, 1) for one in far]
    far_outs = [one if isinstance(one, tuple) else (one, 1, 0) for one in far_outs]
    far_arrays, far_shapes = [one[0] for one in far], [one[0] for one in far_outs]
    counts = [len(args), len(far), len(outs), len(far_outs), len(far), len(far_outs), len(scratch)]

    def body(*refs):
        groups, at = [], 0
        for count in counts:
            groups.append(list(refs[at : at + count]))
            at += count
        near_in, far_in, near_out, far_out, held, leaving, rest = groups
        sems = refs[at]
        used = 0
        arrivals, departures = [], []
        for source, ref, (_, parts) in zip(far_in, held, far):
            arrivals.append(Arriving(source, ref, [sems.at[used + k] for k in range(parts)], parts))
            used += parts
        for target, ref, (_, parts, dim) in zip(far_out, leaving, far_outs):
            departures.append(Leaving(target, ref, [sems.at[used + k] for k in range(parts)], parts, dim))
            used += parts
        kernel(*near_in, *arrivals, *near_out, *departures, *rest)
        for one in arrivals:
            one.ready()
        for one in departures:
            for copy in one.copies:
                copy.wait()

    near_spec, far_spec = pl.BlockSpec(memory_space=pltpu.VMEM), pl.BlockSpec(memory_space=pltpu.HBM)
    moved = sum(a.size * a.dtype.itemsize for a in args + far_arrays + outs + far_shapes)
    return pl.pallas_call(
        body,
        out_shape=tuple(outs + far_shapes),
        in_specs=[near_spec] * len(args) + [far_spec] * len(far),
        out_specs=tuple([near_spec] * len(outs) + [far_spec] * len(far_outs)),
        scratch_shapes=[pltpu.VMEM(a.shape, a.dtype) for a in far_arrays + far_shapes]
        + scratch
        + [pltpu.SemaphoreType.DMA((max(1, sum(one[1] for one in far + far_outs)),))],
        compiler_params=pltpu.CompilerParams(vmem_limit_bytes=int(room * 2**20)),
        cost_estimate=pl.CostEstimate(flops=flops, bytes_accessed=moved, transcendentals=0),
    )(*args, *far_arrays)


def by_channel(pair, cotangent, valid, in_gain, proj_weight, gate_weight, out_gain, out_weight):
    tile, _, channels = pair.shape
    hidden = out_weight.shape[0]
    cells = tile * tile
    grid_rows = lax.axis_size("row")
    devices = grid_rows * lax.axis_size("col")
    per = hidden // devices
    n = tile * grid_rows
    shape = lambda dims, dtype: jax.ShapeDtypeStruct(dims, dtype)
    exchange = lambda x, order: lax.all_to_all(x, ("row", "col"), 0, 0, axis_index_groups=[order], tiled=True)
    flat = pair.reshape(cells, channels)
    flat_cot = cotangent.reshape(cells, channels)
    valid_row = valid.reshape(1, -1)
    in_row = in_gain.reshape(1, -1)
    out_row = out_gain.reshape(1, -1)
    both = 2 * per
    plane = shape((channels, cells), F32)

    (sides,) = call(
        functools.partial(project_kernel, tile, 4),
        [],
        (),
        2 * cells * channels * 4 * hidden,
        far=(flat, proj_weight, valid_row, in_row),
        far_outs=[(shape((devices, both, cells), BF16), 4, 0)],
        room=62,
    )
    sides, flat_2, flat_cot_2 = lax.optimization_barrier((sides, flat, flat_cot))
    sides = exchange(sides, FIRST)
    (q,) = call(
        gate_kernel,
        [plane],
        (),
        2 * cells * channels * 2 * hidden,
        far=(flat_2, flat_cot_2, in_row, gate_weight, out_row, out_weight),
    )
    sides, q = lax.optimization_barrier((sides, q))
    tri, left, right = call(
        functools.partial(tri_kernel, grid_rows),
        [shape((devices, both, cells // 2), BF16), shape((per, n, n), BF16), shape((per, n, n), BF16)],
        (sides,),
        2 * per * n * n * n,
        [pltpu.VMEM((n * both, n), F32), pltpu.VMEM((n * per, n), F32)],
    )
    tri = exchange(tri, LATER)
    (d_tri,) = call(
        d_tri_kernel,
        [shape((devices, both, cells // 2), BF16)],
        (tri, q),
        20 * cells * hidden,
    )
    d_tri = exchange(d_tri, LATER)
    (d_sides,) = call(
        functools.partial(sides_kernel, grid_rows),
        [],
        (d_tri, left, right),
        4 * per * n * n * n,
        [pltpu.VMEM((n * per, n), F32), pltpu.VMEM((n * both, n), F32)],
        far_outs=[(shape((devices, both, cells), BF16), devices, 0)],
    )
    d_sides, flat_4, flat_cot_4, tri = lax.optimization_barrier((d_sides, flat, flat_cot, tri))
    d_sides = exchange(d_sides, LATER)
    unit, inv, factors, update = call(
        functools.partial(update_kernel, tile),
        [plane, shape((1, cells), F32), shape((5, hidden, cells), BF16)],
        (),
        2 * cells * channels * 6 * hidden,
        far=(tri, out_row, out_weight, flat_4, flat_cot_4, valid_row, in_row, gate_weight, proj_weight),
        far_outs=[shape((cells, channels), BF16)],
    )
    (pair_grad,) = call(
        functools.partial(pair_grad_kernel, 4),
        [],
        (d_sides, factors, unit, inv),
        2 * cells * channels * 5 * hidden,
        far=(in_row, proj_weight, gate_weight),
        far_outs=[(shape((cells, channels), F32), 4, 0)],
    )
    return (update.reshape(pair.shape), pair_grad.reshape(pair.shape))


def fits(pair, out_weight):
    rows, cols = lax.axis_size("row"), lax.axis_size("col")
    tile, tile_cols, channels = pair.shape
    hidden = out_weight.shape[0]
    return (
        rows == cols == 4
        and tile == tile_cols
        and tile * rows == LANES
        and channels == LANES
        and hidden == 8 * rows * cols
    )


def step(pair, cotangent, valid, in_gain, proj_weight, gate_weight, out_gain, out_weight):
    plan = by_channel if fits(pair, out_weight) else on_device
    return plan(pair, cotangent, valid, in_gain, proj_weight, gate_weight, out_gain, out_weight)


def solution(mesh):
    placed = (
        P(("replica", "row"), "col", None),
        P(("replica", "row"), "col", None),
        P("replica"),
        P(),
        P(),
        P(),
        P(),
        P(),
    )
    return jax.shard_map(
        step,
        mesh=mesh,
        in_specs=placed,
        out_specs=(P(("replica", "row"), "col", None), P(("replica", "row"), "col", None)),
        check_vma=False,
    )
```

```python
import functools

import jax
import jax.numpy as jnp
from jax import lax
from jax.experimental import pallas as pl
from jax.experimental.pallas import tpu as pltpu
from jax.sharding import PartitionSpec as P

eps_norm = 1e-05


def layer_norm(values, gain):
    mean_val = jnp.mean(values, axis=-1, keepdims=True)
    centred = values - mean_val
    inv_std = lax.rsqrt(jnp.mean(centred * centred, axis=-1, keepdims=True) + eps_norm)
    unit = centred * inv_std
    return (unit * gain, unit, inv_std)


def norm_back(grad_unit, unit, inv_std):
    first = jnp.mean(grad_unit, axis=-1, keepdims=True)
    second = jnp.mean(grad_unit * unit, axis=-1, keepdims=True)
    return inv_std * (grad_unit - first - unit * second)


def on_device(pair, cotangent, valid, in_gain, proj_weight, gate_weight, out_gain, out_weight):
    tile_rows = pair.shape[0]
    channels = pair.shape[2]
    hidden = out_weight.shape[0]
    cells = tile_rows * tile_rows
    keeper = valid.astype(jnp.float32)
    row_keep = lax.dynamic_slice_in_dim(keeper, lax.axis_index("row") * tile_rows, tile_rows)
    col_keep = lax.dynamic_slice_in_dim(keeper, lax.axis_index("col") * tile_rows, tile_rows)
    pair_keep = (row_keep[:, None] * col_keep[None, :])[:, :, None]
    normed_f, unit_in, inv_in = layer_norm(pair.astype(jnp.float32), in_gain)
    normed = normed_f.astype(jnp.bfloat16)
    flat = normed.reshape(cells, channels)
    proj = jnp.dot(flat, proj_weight, preferred_element_type=jnp.float32).reshape(
        tile_rows, tile_rows, 4 * hidden
    )
    left_sig = jax.nn.sigmoid(proj[..., :hidden])
    left_val = proj[..., hidden : 2 * hidden]
    right_sig = jax.nn.sigmoid(proj[..., 2 * hidden : 3 * hidden])
    right_val = proj[..., 3 * hidden :]
    left = (left_sig * left_val * pair_keep).astype(jnp.bfloat16)
    right = (right_sig * right_val * pair_keep).astype(jnp.bfloat16)
    panel = lax.all_gather(right, "row", axis=0, tiled=True)
    piece = panel
    tri = jnp.swapaxes(
        lax.psum_scatter(
            jnp.einsum("ikh,jkh->jih", left, piece, preferred_element_type=jnp.float32),
            "col",
            scatter_dimension=0,
            tiled=True,
        ),
        0,
        1,
    )
    tnorm_f, unit_tri, inv_tri = layer_norm(tri, out_gain)
    tnorm = tnorm_f.astype(jnp.bfloat16)
    gate = jax.nn.sigmoid(jnp.dot(flat, gate_weight, preferred_element_type=jnp.float32)).reshape(
        tile_rows, tile_rows, channels
    )
    lin = jnp.dot(
        tnorm.reshape(cells, hidden), out_weight, preferred_element_type=jnp.float32
    ).reshape(tile_rows, tile_rows, channels)
    update = (gate * lin).astype(jnp.bfloat16)
    cot = cotangent.astype(jnp.float32)
    d_lin = (cot * gate).astype(jnp.bfloat16)
    d_gpre = (cot * lin * gate * (1.0 - gate)).astype(jnp.bfloat16)
    d_tnorm = jnp.dot(
        d_lin.reshape(cells, channels), out_weight.T, preferred_element_type=jnp.float32
    ).reshape(tile_rows, tile_rows, hidden)
    d_tri = norm_back(d_tnorm * out_gain, unit_tri, inv_tri).astype(jnp.bfloat16)
    grad_rows = lax.all_gather(d_tri, "col", axis=1, tiled=True)
    back_panel = lax.all_gather(right, "row", axis=0, tiled=True)
    piece = grad_rows
    d_right = lax.psum_scatter(
        jnp.einsum("ijh,ikh->jkh", piece, left, preferred_element_type=jnp.float32),
        "row",
        scatter_dimension=0,
        tiled=True,
    )
    d_left = jnp.einsum("ijh,jkh->ikh", grad_rows, back_panel, preferred_element_type=jnp.float32)
    d_proj = jnp.concatenate(
        [
            d_left * pair_keep * left_val * left_sig * (1.0 - left_sig),
            d_left * pair_keep * left_sig,
            d_right * pair_keep * right_val * right_sig * (1.0 - right_sig),
            d_right * pair_keep * right_sig,
        ],
        axis=-1,
    ).astype(jnp.bfloat16)
    d_normed = jnp.dot(
        d_proj.reshape(cells, 4 * hidden), proj_weight.T, preferred_element_type=jnp.float32
    )
    d_normed = d_normed + jnp.dot(
        d_gpre.reshape(cells, channels), gate_weight.T, preferred_element_type=jnp.float32
    )
    pair_grad = norm_back(
        d_normed.reshape(tile_rows, tile_rows, channels) * in_gain, unit_in, inv_in
    )
    return (update, pair_grad)


F32 = jnp.float32
BF16 = jnp.bfloat16
LANES = 128
FIRST = (14, 15, 3, 4, 13, 10, 11, 12, 6, 0, 9, 2, 1, 5, 8, 7)
LATER = (14, 15, 3, 4, 13, 10, 11, 12, 6, 0, 9, 2, 1, 5, 8, 7)
FIRST_PLACE = tuple(FIRST.index(device) for device in range(len(FIRST)))
LATER_PLACE = tuple(LATER.index(device) for device in range(len(LATER)))
HOLDER = tuple(LATER.index(device) for device in FIRST)


def dot(a, b, dims):
    return lax.dot_general(a, b, ((dims[:1], dims[1:]), ((), ())), preferred_element_type=F32)


def column(gain):
    n = gain.shape[1]
    return jnp.broadcast_to(gain, (n, n)).T


def spread(col, width):
    return jnp.concatenate([col] * (width // col.shape[1]), axis=1)


def unit_rows(values):
    n = values.shape[0]
    centred = values - jnp.sum(values, axis=0, keepdims=True) * (1.0 / n)
    inv = lax.rsqrt(jnp.sum(centred * centred, axis=0, keepdims=True) * (1.0 / n) + eps_norm)
    return centred * inv, inv


def unit_back(q, unit, inv):
    n = q.shape[0]
    first = jnp.sum(q, axis=0, keepdims=True) * (1.0 / n)
    second = jnp.sum(q * unit, axis=0, keepdims=True) * (1.0 / n)
    return inv * (q - first - unit * second)


def one_hot(at):
    return jnp.where(at, 1.0, 0.0).astype(BF16)


def block_swap():
    width = LANES // 4
    row = lax.broadcasted_iota(jnp.int32, (width, LANES), 0)
    lane = lax.broadcasted_iota(jnp.int32, (width, LANES), 1)
    none = jnp.zeros((width, LANES), BF16)
    to = [one_hot(row + width * c == lane) for c in range(4)]
    return jnp.concatenate(
        [jnp.concatenate([to[c] if n == p else none for n in range(4)], axis=1) for c in range(4) for p in range(4)],
        axis=0,
    )


def keep_row(valid, tile, cells):
    n = valid.ref.shape[1]
    groups, rows = cells // n, n // tile
    token = lax.broadcasted_iota(jnp.int32, (n, n), 0)
    lane = lax.broadcasted_iota(jnp.int32, (n, n), 1)
    place = lax.broadcasted_iota(jnp.int32, (groups, n), 1) - lax.axis_index("row") * tile
    group = rows * lax.broadcasted_iota(jnp.int32, (groups, n), 0)
    inside = jnp.logical_and(place >= group, place < group + rows)
    first = one_hot(lax.rem(token, rows) == lax.div(lane, tile))
    second = one_hot(token - lax.axis_index("col") * tile == lax.rem(lane, tile))
    v = jnp.broadcast_to(valid.ready()[...].astype(F32), (groups, n))
    own = jnp.where(inside, v, 0.0).astype(BF16)
    keep = dot(own, first, (1, 0)) * dot(v.astype(BF16), second, (1, 0))
    return jnp.concatenate([keep[g : g + 1] for g in range(groups)], axis=1)


def normed_of(pair, in_gain):
    unit, inv = unit_rows(pair.ready()[...].astype(F32).T)
    normed = (unit * spread(column(in_gain.ready()[...]), unit.shape[1])).astype(BF16)
    return normed, unit, inv


def project_kernel(tile, parts, pair, proj_weight, valid, in_gain, out):
    cells, channels = pair.ref.shape
    hidden = proj_weight.ref.shape[1] // 4
    shards, both, _ = out.ref.shape
    per = both // 2
    keep = keep_row(valid, tile, cells)
    normed, _, _ = normed_of(pair, in_gain)
    weights = proj_weight.ready()[...].T
    share = hidden // parts
    for part in range(parts):
        rows = [weights[block * hidden + part * share : block * hidden + (part + 1) * share] for block in range(4)]
        proj = dot(jnp.concatenate(rows, axis=0), normed, (1, 0))
        left = jax.nn.sigmoid(proj[:share]) * proj[share : 2 * share] * keep
        right = jax.nn.sigmoid(proj[2 * share : 3 * share]) * proj[3 * share :] * keep
        for s in range(shards // parts):
            own = slice(s * per, (s + 1) * per)
            out.ref[part * shards // parts + s] = jnp.concatenate([left[own], right[own]], axis=0).astype(BF16)
        out.send(part)


def gate_of(normed, cot, gate_weight):
    gate = jax.nn.sigmoid(dot(gate_weight.ready()[...].T, normed, (1, 0)))
    return gate, cot.ready()[...].astype(F32).T


def gate_kernel(pair, cot, in_gain, gate_weight, out_gain, out_weight, q_ref):
    normed, _, _ = normed_of(pair, in_gain)
    gate, cot_rows = gate_of(normed, cot, gate_weight)
    q = dot(out_weight.ready()[...], (cot_rows * gate).astype(BF16), (1, 0))
    q_ref[...] = q * spread(column(out_gain.ready()[...]), q.shape[1])


def tri_kernel(grid_rows, recv_ref, out_ref, left_ref, right_ref, rows, tri):
    devices, both, cells = recv_ref.shape
    per = both // 2
    n = left_ref.shape[1]
    tile = n // grid_rows
    groups = cells // LANES
    swap = block_swap()
    for r in range(grid_rows):
        x = jnp.concatenate(
            [
                jnp.concatenate(
                    [recv_ref[FIRST_PLACE[grid_rows * r + c], :, g * LANES : (g + 1) * LANES] for c in range(grid_rows)], axis=1
                )
                for g in range(groups)
            ],
            axis=0,
        )
        y = dot(x, swap, (1, 0))
        for g in range(groups):
            for p in range(grid_rows):
                at = (r * tile + g * grid_rows + p) * both
                rows[at : at + both, :] = y[g * both : (g + 1) * both, p * LANES : (p + 1) * LANES]
    for h in range(per):
        left = rows[pl.ds(h, n, stride=both), :].astype(BF16)
        right = rows[pl.ds(per + h, n, stride=both), :].astype(BF16)
        left_ref[h] = left
        right_ref[h] = right
        tri[pl.ds(h, n, stride=per), :] = dot(left, right, (1, 1))
    half = groups // 2
    for r in range(grid_rows):
        x = jnp.concatenate(
            [
                jnp.concatenate(
                    [
                        tri[at : at + per, :]
                        for p in range(grid_rows)
                        for at in [(r * tile + (g + k * half) * grid_rows + p) * per]
                    ],
                    axis=1,
                )
                for g in range(half)
                for k in range(2)
            ],
            axis=0,
        )
        y = dot(x.astype(BF16), swap, (1, 0)).astype(BF16)
        for g in range(half):
            for c in range(grid_rows):
                out_ref[LATER_PLACE[grid_rows * r + c], :, g * LANES : (g + 1) * LANES] = y[
                    g * both : (g + 1) * both, c * LANES : (c + 1) * LANES
                ]


def halves_of(recv_ref):
    per = recv_ref.shape[1] // 2
    blocks = [recv_ref[holder].astype(F32) for holder in HOLDER]
    return jnp.concatenate(
        [jnp.concatenate([b[k * per : (k + 1) * per] for b in blocks], axis=0) for k in range(2)], axis=1
    )


def d_tri_kernel(recv_ref, q_ref, out_ref):
    _, both, width = recv_ref.shape
    per = both // 2
    unit, inv = unit_rows(halves_of(recv_ref))
    d_tri = unit_back(q_ref[...], unit, inv)
    for shard, holder in enumerate(HOLDER):
        rows = d_tri[shard * per : (shard + 1) * per]
        out_ref[holder] = jnp.concatenate([rows[:, :width], rows[:, width:]], axis=0).astype(BF16)


def update_kernel(
    tile, tri, out_gain, out_weight, pair, cot, valid, in_gain, gate_weight, proj_weight,
    unit_ref, inv_ref, factor_ref, update,
):
    normed, unit, inv = normed_of(pair, in_gain)
    unit_ref[...] = unit
    inv_ref[...] = inv
    gate, cot_rows = gate_of(normed, cot, gate_weight)
    unit_tri, _ = unit_rows(halves_of(tri.ready()))
    tnorm = (unit_tri * spread(column(out_gain.ready()[...]), unit.shape[1])).astype(BF16)
    lin = dot(out_weight.ready()[...].T, tnorm, (1, 0))
    update.ref[...] = (gate * lin).T.astype(BF16)
    update.send()
    factor_ref[4] = (cot_rows * lin * gate * (1.0 - gate)).astype(BF16)
    hidden = proj_weight.ref.shape[1] // 4
    keep = keep_row(valid, tile, unit.shape[1])
    weights = proj_weight.ready()
    for side in range(2):
        weight = weights[:, 2 * hidden * side : 2 * hidden * (side + 1)].T
        proj = dot(weight, normed, (1, 0))
        sig = jax.nn.sigmoid(proj[:hidden])
        factor_ref[2 * side] = (keep * proj[hidden:] * sig * (1.0 - sig)).astype(BF16)
        factor_ref[2 * side + 1] = (keep * sig).astype(BF16)


def sides_kernel(grid_rows, recv_ref, left_ref, right_ref, out, d_tri, rows):
    devices, both, cells = out.ref.shape
    per = both // 2
    n = left_ref.shape[1]
    tile = n // grid_rows
    groups = cells // LANES
    half = groups // 2
    swap = block_swap()
    for r in range(grid_rows):
        x = jnp.concatenate(
            [
                jnp.concatenate(
                    [recv_ref[LATER_PLACE[grid_rows * r + c], :, g * LANES : (g + 1) * LANES] for c in range(grid_rows)], axis=1
                )
                for g in range(half)
            ],
            axis=0,
        )
        y = dot(x, swap, (1, 0))
        for g in range(half):
            for k in range(2):
                for p in range(grid_rows):
                    at = (r * tile + (g + k * half) * grid_rows + p) * per
                    d_tri[at : at + per, :] = y[
                        g * both + k * per : g * both + (k + 1) * per, p * LANES : (p + 1) * LANES
                    ]
    for h in range(per):
        grad = d_tri[pl.ds(h, n, stride=per), :].astype(BF16)
        rows[pl.ds(h, n, stride=both), :] = dot(grad, right_ref[h], (1, 0))
        rows[pl.ds(per + h, n, stride=both), :] = dot(grad, left_ref[h], (0, 0))
    for r in range(grid_rows):
        x = jnp.concatenate(
            [
                jnp.concatenate(
                    [
                        rows[at : at + both, :]
                        for p in range(grid_rows)
                        for at in [(r * tile + g * grid_rows + p) * both]
                    ],
                    axis=1,
                )
                for g in range(groups)
            ],
            axis=0,
        )
        y = dot(x.astype(BF16), swap, (1, 0)).astype(BF16)
        for c in range(grid_rows):
            place = LATER_PLACE[grid_rows * r + c]
            for g in range(groups):
                out.ref[place, :, g * LANES : (g + 1) * LANES] = y[
                    g * both : (g + 1) * both, c * LANES : (c + 1) * LANES
                ]
            out.send(place)


def pair_grad_kernel(parts, recv_ref, factor_ref, unit_ref, inv_ref, in_gain, proj_weight, gate_weight, out):
    _, both, cells = recv_ref.shape
    width = cells // parts
    gain = spread(column(in_gain.ready()[...]), width)
    weights, gate_weights = proj_weight.ready()[...], gate_weight.ready()[...]
    for part in range(parts):
        lanes = slice(part * width, (part + 1) * width)
        blocks = [recv_ref[holder, :, lanes].astype(F32) for holder in HOLDER]
        grads = [
            jnp.concatenate([b[k * both // 2 : (k + 1) * both // 2] for b in blocks], axis=0) for k in range(2)
        ]
        d_proj = jnp.concatenate(
            [
                (grad * factor_ref[2 * side + k, :, lanes].astype(F32)).astype(BF16)
                for side, grad in enumerate(grads)
                for k in range(2)
            ],
            axis=0,
        )
        d_normed = dot(weights, d_proj, (1, 0)) + dot(gate_weights, factor_ref[4, :, lanes], (1, 0))
        out.ref[lanes, :] = unit_back(d_normed * gain, unit_ref[:, lanes], inv_ref[:, lanes]).T
        out.send(part)


class Arriving:
    def __init__(self, source, ref, sems, parts):
        size = ref.shape[0] // parts
        cuts = [pl.ds(part * size, size) for part in range(parts)]
        self.ref = ref
        self.copies = [pltpu.make_async_copy(source.at[cut], ref.at[cut], sem) for cut, sem in zip(cuts, sems)]
        for copy in self.copies:
            copy.start()
        self.waiting = set(range(parts))

    def ready(self, part=None):
        for one in sorted(self.waiting) if part is None else [part]:
            if one in self.waiting:
                self.copies[one].wait()
                self.waiting.remove(one)
        return self.ref


class Leaving:
    def __init__(self, target, ref, sems, parts, dim):
        size = ref.shape[dim] // parts
        cuts = [(slice(None),) * dim + (pl.ds(part * size, size),) for part in range(parts)]
        self.ref = ref
        self.copies = [pltpu.make_async_copy(ref.at[cut], target.at[cut], sem) for cut, sem in zip(cuts, sems)]

    def send(self, part=0):
        self.copies[part].start()


def call(kernel, outs, args, flops, scratch=(), far=(), far_outs=(), room=24):
    outs, args, scratch = list(outs), list(args), list(scratch)
    far = [one if isinstance(one, tuple) else (one, 1) for one in far]
    far_outs = [one if isinstance(one, tuple) else (one, 1, 0) for one in far_outs]
    far_arrays, far_shapes = [one[0] for one in far], [one[0] for one in far_outs]
    counts = [len(args), len(far), len(outs), len(far_outs), len(far), len(far_outs), len(scratch)]

    def body(*refs):
        groups, at = [], 0
        for count in counts:
            groups.append(list(refs[at : at + count]))
            at += count
        near_in, far_in, near_out, far_out, held, leaving, rest = groups
        sems = refs[at]
        used = 0
        arrivals, departures = [], []
        for source, ref, (_, parts) in zip(far_in, held, far):
            arrivals.append(Arriving(source, ref, [sems.at[used + k] for k in range(parts)], parts))
            used += parts
        for target, ref, (_, parts, dim) in zip(far_out, leaving, far_outs):
            departures.append(Leaving(target, ref, [sems.at[used + k] for k in range(parts)], parts, dim))
            used += parts
        kernel(*near_in, *arrivals, *near_out, *departures, *rest)
        for one in arrivals:
            one.ready()
        for one in departures:
            for copy in one.copies:
                copy.wait()

    near_spec, far_spec = pl.BlockSpec(memory_space=pltpu.VMEM), pl.BlockSpec(memory_space=pltpu.HBM)
    moved = sum(a.size * a.dtype.itemsize for a in args + far_arrays + outs + far_shapes)
    return pl.pallas_call(
        body,
        out_shape=tuple(outs + far_shapes),
        in_specs=[near_spec] * len(args) + [far_spec] * len(far),
        out_specs=tuple([near_spec] * len(outs) + [far_spec] * len(far_outs)),
        scratch_shapes=[pltpu.VMEM(a.shape, a.dtype) for a in far_arrays + far_shapes]
        + scratch
        + [pltpu.SemaphoreType.DMA((max(1, sum(one[1] for one in far + far_outs)),))],
        compiler_params=pltpu.CompilerParams(vmem_limit_bytes=int(room * 2**20)),
        cost_estimate=pl.CostEstimate(flops=flops, bytes_accessed=moved, transcendentals=0),
    )(*args, *far_arrays)


def by_channel(pair, cotangent, valid, in_gain, proj_weight, gate_weight, out_gain, out_weight):
    tile, _, channels = pair.shape
    hidden = out_weight.shape[0]
    cells = tile * tile
    grid_rows = lax.axis_size("row")
    devices = grid_rows * lax.axis_size("col")
    per = hidden // devices
    n = tile * grid_rows
    shape = lambda dims, dtype: jax.ShapeDtypeStruct(dims, dtype)
    exchange = lambda x, order: lax.all_to_all(x, ("row", "col"), 0, 0, axis_index_groups=[order], tiled=True)
    flat = pair.reshape(cells, channels)
    flat_cot = cotangent.reshape(cells, channels)
    valid_row = valid.reshape(1, -1)
    in_row = in_gain.reshape(1, -1)
    out_row = out_gain.reshape(1, -1)
    both = 2 * per
    plane = shape((channels, cells), F32)

    (sides,) = call(
        functools.partial(project_kernel, tile, 4),
        [],
        (),
        2 * cells * channels * 4 * hidden,
        far=(flat, proj_weight, valid_row, in_row),
        far_outs=[(shape((devices, both, cells), BF16), 4, 0)],
        room=62,
    )
    sides, flat_2, flat_cot_2 = lax.optimization_barrier((sides, flat, flat_cot))
    sides = exchange(sides, FIRST)
    (q,) = call(
        gate_kernel,
        [plane],
        (),
        2 * cells * channels * 2 * hidden,
        far=(flat_2, flat_cot_2, in_row, gate_weight, out_row, out_weight),
    )
    sides, q = lax.optimization_barrier((sides, q))
    tri, left, right = call(
        functools.partial(tri_kernel, grid_rows),
        [shape((devices, both, cells // 2), BF16), shape((per, n, n), BF16), shape((per, n, n), BF16)],
        (sides,),
        2 * per * n * n * n,
        [pltpu.VMEM((n * both, n), F32), pltpu.VMEM((n * per, n), F32)],
    )
    tri = exchange(tri, LATER)
    (d_tri,) = call(
        d_tri_kernel,
        [shape((devices, both, cells // 2), BF16)],
        (tri, q),
        20 * cells * hidden,
    )
    d_tri = exchange(d_tri, LATER)
    (d_sides,) = call(
        functools.partial(sides_kernel, grid_rows),
        [],
        (d_tri, left, right),
        4 * per * n * n * n,
        [pltpu.VMEM((n * per, n), F32), pltpu.VMEM((n * both, n), F32)],
        far_outs=[(shape((devices, both, cells), BF16), devices, 0)],
    )
    d_sides, flat_4, flat_cot_4, tri = lax.optimization_barrier((d_sides, flat, flat_cot, tri))
    d_sides = exchange(d_sides, LATER)
    unit, inv, factors, update = call(
        functools.partial(update_kernel, tile),
        [plane, shape((1, cells), F32), shape((5, hidden, cells), BF16)],
        (),
        2 * cells * channels * 6 * hidden,
        far=(tri, out_row, out_weight, flat_4, flat_cot_4, valid_row, in_row, gate_weight, proj_weight),
        far_outs=[shape((cells, channels), BF16)],
    )
    (pair_grad,) = call(
        functools.partial(pair_grad_kernel, 4),
        [],
        (d_sides, factors, unit, inv),
        2 * cells * channels * 5 * hidden,
        far=(in_row, proj_weight, gate_weight),
        far_outs=[(shape((cells, channels), F32), 4, 0)],
    )
    return (update.reshape(pair.shape), pair_grad.reshape(pair.shape))


def fits(pair, out_weight):
    rows, cols = lax.axis_size("row"), lax.axis_size("col")
    tile, tile_cols, channels = pair.shape
    hidden = out_weight.shape[0]
    return (
        rows == cols == 4
        and tile == tile_cols
        and tile * rows == LANES
        and channels == LANES
        and hidden == 8 * rows * cols
    )


def step(pair, cotangent, valid, in_gain, proj_weight, gate_weight, out_gain, out_weight):
    plan = by_channel if fits(pair, out_weight) else on_device
    return plan(pair, cotangent, valid, in_gain, proj_weight, gate_weight, out_gain, out_weight)


def solution(mesh):
    placed = (
        P(("replica", "row"), "col", None),
        P(("replica", "row"), "col", None),
        P("replica"),
        P(),
        P(),
        P(),
        P(),
        P(),
    )
    return jax.shard_map(
        step,
        mesh=mesh,
        in_specs=placed,
        out_specs=(P(("replica", "row"), "col", None), P(("replica", "row"), "col", None)),
        check_vma=False,
    )
```
